256 devices in a mesh: mass: 8 (over x, core), seq: 32 (over y, z).
Axes of the slice: x: 4, y: 4, z: 8, core: 2. Of those that a mesh axis runs over, the one named last changes fastest.
Arguments:
- peptide_tokens: int32 [16384, 32], P(('mass', 'seq')), may hold values from 0 to 31
- peptide_lengths: int32 [16384], P(('mass', 'seq')), may hold values from 7 to 32
- target_owner: int32 [16384, 1], P(('mass', 'seq')), may hold values from 0 to 7; in each aligned block of 64 rows (0 to 63, 64 to 127, ...) at most 16 rows name the same one
- target_sub: int32 [16384], P(('mass', 'seq')), may hold values from 0 to 255
- decoy_owner: int32 [16384, 1], P(('mass', 'seq')), may hold values from 0 to 7; in each aligned block of 64 rows (0 to 63, 64 to 127, ...) at most 16 rows name the same one
- decoy_sub: int32 [16384], P(('mass', 'seq')), may hold values from 0 to 255
- embedding: bfloat16 [32, 256], replicated, may hold values from -6 to 6
- w_qkv: bfloat16 [2, 256, 768], replicated, may hold values from -2 to 2
- w_out: bfloat16 [2, 256, 256], replicated, may hold values from -0.375 to 0.375
- w_up: bfloat16 [2, 256, 1024], replicated, may hold values from -0.375 to 0.375
- w_down: bfloat16 [2, 1024, 256], replicated, may hold values from -0.1875 to 0.1875
- layer_gain: bfloat16 [2, 2, 256], replicated, may hold values from 0.5 to 1.5
- final_gain: bfloat16 [256], replicated, may hold values from 0.5 to 1.5
- w_head: bfloat16 [256, 32], replicated, may hold values from -0.375 to 0.375
- query_spectra: bfloat16 [8192, 1024], P(('mass', 'seq')), may hold values from -6 to 6
- query_bin: int32 [8192], P(('mass', 'seq')), may hold values from 0 to 2047, as said below
Outputs:
- target_best: float32 [8192], P(('mass', 'seq'))
- decoy_best: float32 [8192], P(('mass', 'seq'))
The draws below stay inside these ranges and needn't reach their ends.
Inputs may be any that keep to these rules, and one draw needn't show every extreme that they name: `target_owner`: among the rows of one device at most 16 name the same owner. `decoy_owner`: among the rows of one device at most 16 name the same owner. `query_bin`: queries d * 32 to (d + 1) * 32 - 1 hold the bins d * 8 to (d + 1) * 8 - 1, each exactly 4 times.
All inputs are finite; a program needn't handle non-finite values.
Results may differ from the reference program's by a relative error of at most 0.0055.
Values may be sent and summed in bfloat16 or wider, within the bound.
No kernel may reach another device: no remote copies, remote signals or barrier semaphores. Data moves between devices by JAX's collectives and lax.ppermute only.
A program may use at most 128 MiB of HBM per device.

```python
import math
import jax
import jax.numpy as jnp
import numpy as np
from jax import lax

D = 256
HEADS = 8
FF = 1024
VOCAB = 32
L = 32
ION = 32
NL = 2
QPB = 4
PEP_DEV = 64
Q_DEV = 32
SPEC = 1024
CAP = 16
PEPTIDES = 16384
QUERIES = 8192
BIN_SEQ = 8
BIN_DEV = 256
BINS = 2048
N_MASS = 8
DEVICES = 256


def draw_w_qkv(key, part):
    key = jax.random.fold_in(key, 11)
    key_query, key_key, key_value = jax.random.split(key, 3)
    base = jax.random.normal(key_query, (NL, D, D), jnp.float32) / math.sqrt(D)
    other = jax.random.normal(key_key, (NL, D, D), jnp.float32) / math.sqrt(D)
    value = jax.random.normal(key_value, (NL, D, D), jnp.float32) / math.sqrt(D)
    query = base
    keys = other
    whole = jnp.concatenate([query, keys, value], axis=2)
    return jnp.clip(whole, -2.0, 2.0).astype(jnp.bfloat16)


def draw_query_bin(key, part):
    key = jax.random.fold_in(key, 23)
    device_keys = jax.random.split(key, DEVICES)
    base = jnp.arange(Q_DEV, dtype=jnp.int32) // QPB

    def shuffle(device_key):
        return jax.random.permutation(device_key, base)
    mixed = jax.vmap(shuffle)(device_keys)
    offset = jnp.arange(DEVICES, dtype=jnp.int32)[:, None] * BIN_SEQ
    return (mixed + offset).reshape(QUERIES).astype(jnp.int32)


def touch_ends(array, key, smallest, largest):
    extent = array.shape
    spot = [jax.random.randint(jax.random.fold_in(key, axis), (), 0, extent[axis]) for axis in range(len(extent))]
    array = array.at[tuple(spot)].set(smallest)
    longest = extent.index(max(extent))
    spot[longest] = (spot[longest] + 1) % extent[longest]
    return array.at[tuple(spot)].set(largest)


def shard_levels(key, extent, cuts, low, largest):
    def one(dim, blocks):
        steps = jax.random.uniform(jax.random.fold_in(jax.random.fold_in(key, 6), dim), (blocks,), jnp.float32, low / len(cuts), largest / len(cuts))
        return jnp.repeat(jnp.exp(steps), extent[dim] // blocks).reshape((-1,) + (1,) * (len(extent) - dim - 1))

    loudness = one(*cuts[0])
    for cut in cuts[1:]:
        loudness = loudness * one(*cut)
    return loudness


def cumulative_ranks(amount, slope):
    loads = [(1 << 20) // math.isqrt(standing ** slope) + 1 for standing in range(1, amount + 1)]
    scale = 1 + sum(loads) // (1 << 30)
    return np.cumsum(np.array([max(1, weight // scale) for weight in loads]))


def skewed_ids(own_key, shape, amount, lean):
    table = cumulative_ranks(amount, lean)
    pick = jax.random.randint(jax.random.fold_in(own_key, 1), shape, 0, int(table[amount - 1]))
    rank = jnp.searchsorted(jnp.asarray(table, jnp.int32), pick, side="right")
    return jax.random.permutation(jax.random.fold_in(own_key, 2), amount)[rank].astype(jnp.int32)


def deal_out(rng, own, number, rows, number_of, top, bound, slope):
    sequence = jax.random.permutation(rng, number_of)
    heavy_load, usual = portions_of(number_of, rows * top, bound, slope, True), portions_of(number_of, rows * top, bound, slope, False)
    places = jnp.arange(number_of)

    def named(sizes, rotation):
        used = int((sizes > 0).sum())
        fixed = max(1, used // 4)
        shifted = fixed + (places - fixed + rotation * (used - fixed)) % max(1, number_of - fixed)
        return jnp.zeros((number_of,), jnp.int32).at[sequence[jnp.where(places < fixed, places, shifted)]].set(jnp.asarray(sizes, jnp.int32))

    sizes = jnp.where(number % 4 == 0, named(heavy_load, number // 4), named(usual, number - number // 4 - 1))
    mixed = jax.random.permutation(jax.random.fold_in(own, 3), number_of)
    donor, receiver = mixed[0:number_of // 2 * 2:2], mixed[1:number_of // 2 * 2:2]
    slack = jnp.minimum(sizes[donor] - 1, bound - sizes[receiver]) // 2
    slack = jnp.where((donor == sequence[0]) | (receiver == sequence[0]) | (sizes[receiver] == 0), 0, jnp.maximum(slack, 0))
    shifted = jax.random.randint(jax.random.fold_in(own, 4), (number_of // 2,), 0, 1 << 20) % (slack + 1)
    sizes = sizes.at[donor].add(-shifted).at[receiver].add(shifted)
    labels = jnp.searchsorted(jnp.cumsum(sizes), jnp.arange(rows * top), side="right").astype(jnp.int32)
    grid = labels.reshape(top, rows).T
    grid = grid[jax.random.permutation(jax.random.fold_in(own, 1), rows)]
    rotation = jax.random.randint(jax.random.fold_in(own, 2), (rows, 1), 0, top)
    return jnp.take_along_axis(grid, (jnp.arange(top)[None, :] + rotation) % top, axis=1)


def portions_of(count, total, reach, slope, full):
    weights = [(1 << 20) // math.isqrt(rank ** slope) + 1 for rank in range(1, count + 1)]
    largest = reach if full else min(reach, max(-(-total // count), total * weights[0] // sum(weights)))
    least = 1 if total - largest >= count - 1 else 0
    given, spare = [largest] + [least] * (count - 1), total - largest - least * (count - 1)
    while spare > 0:
        movable = [i for i in range(1, count) if given[i] < largest] or [i for i in range(1, count) if given[i] < reach]
        mass, budget = sum([weights[i] for i in movable]), spare
        for i in movable:
            more = min(reach - given[i], max(1, budget * weights[i] // mass), spare)
            given[i] = given[i] + more
            spare = spare - more
    return np.array(given)


def noise(own_key, dims, deviation, most, cuts=(), kind=jnp.bfloat16):
    values = deviation * jax.random.normal(own_key, dims, jnp.float32)
    if cuts:
        values = values * shard_levels(own_key, dims, cuts, -0.22, 0.18)
    return jnp.clip(values, -most, most).astype(kind)


def setup_inputs(seed: int = 0) -> dict:
    arg_keys = jax.random.split(jax.random.key(seed), 17)
    peptide_tokens = touch_ends(skewed_ids(arg_keys[0], (PEPTIDES, L), VOCAB, 1), jax.random.fold_in(arg_keys[0], 3), 0, VOCAB - 1).astype(jnp.int32)
    peptide_lengths = touch_ends(jax.random.randint(arg_keys[1], (PEPTIDES,), 7, L + 1), jax.random.fold_in(arg_keys[1], 1), 7, L).astype(jnp.int32)
    target_owner_keys = jax.random.split(jax.random.fold_in(arg_keys[2], 1), PEPTIDES // PEP_DEV)
    target_owner_turns = jax.random.permutation(jax.random.fold_in(arg_keys[2], 3), PEPTIDES // PEP_DEV)
    target_owner = jax.vmap(lambda own, number: deal_out(jax.random.fold_in(arg_keys[2], 2), own, number, PEP_DEV, N_MASS, 1, CAP, 2))(target_owner_keys, target_owner_turns).reshape((PEPTIDES, 1))
    target_sub = touch_ends(jax.random.randint(arg_keys[3], (PEPTIDES,), 0, BIN_DEV), jax.random.fold_in(arg_keys[3], 1), 0, BIN_DEV - 1).astype(jnp.int32)
    decoy_owner_keys = jax.random.split(jax.random.fold_in(arg_keys[4], 1), PEPTIDES // PEP_DEV)
    decoy_owner_turns = jax.random.permutation(jax.random.fold_in(arg_keys[4], 3), PEPTIDES // PEP_DEV)
    decoy_owner = jax.vmap(lambda own, number: deal_out(jax.random.fold_in(arg_keys[4], 2), own, number, PEP_DEV, N_MASS, 1, CAP, 2))(decoy_owner_keys, decoy_owner_turns).reshape((PEPTIDES, 1))
    decoy_sub = touch_ends(jax.random.randint(arg_keys[5], (PEPTIDES,), 0, BIN_DEV), jax.random.fold_in(arg_keys[5], 1), 0, BIN_DEV - 1).astype(jnp.int32)
    embedding = noise(arg_keys[6], (VOCAB, D), 1.0, 6.0)
    w_qkv = draw_w_qkv(jax.random.fold_in(arg_keys[16], 71), 0)
    w_out = noise(arg_keys[8], (NL, D, D), D ** -0.5, 0.375)
    w_up = noise(arg_keys[9], (NL, D, FF), D ** -0.5, 0.375)
    w_down = noise(arg_keys[10], (NL, FF, D), FF ** -0.5, 0.1875)
    layer_gain = jnp.clip(1.0 + 0.1 * jax.random.normal(arg_keys[11], (NL, 2, D), jnp.float32), 0.5, 1.5).astype(jnp.bfloat16)
    final_gain = jnp.clip(1.0 + 0.1 * jax.random.normal(arg_keys[12], (D,), jnp.float32), 0.5, 1.5).astype(jnp.bfloat16)
    w_head = noise(arg_keys[13], (D, ION), D ** -0.5, 0.375)
    query_spectra = noise(arg_keys[14], (QUERIES, SPEC), 1.0, 6.0, ((0, 256),))
    query_bin = draw_query_bin(jax.random.fold_in(arg_keys[16], 71), 0)
    return {"peptide_tokens": peptide_tokens, "peptide_lengths": peptide_lengths, "target_owner": target_owner, "target_sub": target_sub, "decoy_owner": decoy_owner, "decoy_sub": decoy_sub, "embedding": embedding, "w_qkv": w_qkv, "w_out": w_out, "w_up": w_up, "w_down": w_down, "layer_gain": layer_gain, "final_gain": final_gain, "w_head": w_head, "query_spectra": query_spectra, "query_bin": query_bin}


EPS = 1e-06

def sinusoid(length, width):
    place = jnp.arange(length, dtype=jnp.float32)[:, None]
    index = jnp.arange(width // 2, dtype=jnp.float32)[None, :]
    angle = place * jnp.exp(-math.log(10000.0) * 2.0 * index / width)
    return jnp.concatenate([jnp.sin(angle), jnp.cos(angle)], axis=1)

def norm_rows(values, gain):
    return values * lax.rsqrt(lax.optimization_barrier(jnp.mean(values * values, axis=-1, keepdims=True)) + EPS) * gain.astype(jnp.float32)

def standardize(spectra):
    centred = spectra - lax.optimization_barrier(jnp.mean(spectra, axis=-1, keepdims=True))
    return (centred * lax.rsqrt(lax.optimization_barrier(jnp.mean(centred * centred, axis=-1, keepdims=True)) + EPS)).astype(jnp.bfloat16)

def predict_block(tokens, lengths, embedding, w_qkv, w_out, w_up, w_down, layer_gain, final_gain, w_head):
    count, length = tokens.shape
    vocab, width = embedding.shape
    size = width // HEADS
    onehot = (tokens.reshape(-1)[:, None] == jnp.arange(vocab, dtype=jnp.int32)[None, :]).astype(jnp.bfloat16)
    state = jnp.dot(onehot, embedding, preferred_element_type=jnp.float32).reshape(count, length, width)
    state = (state + sinusoid(length, width)[None]).reshape(count * length, width)
    valid = jnp.arange(length, dtype=jnp.int32)[None, :] < lengths[:, None]
    for layer in range(NL):
        normed = norm_rows(state, layer_gain[layer, 0]).astype(jnp.bfloat16)
        mixed = jnp.dot(normed, w_qkv[layer], preferred_element_type=jnp.float32).astype(jnp.bfloat16)
        mixed = mixed.reshape(count, length, 3, HEADS, size)
        query = mixed[:, :, 0].astype(jnp.float32)
        keys = mixed[:, :, 1].astype(jnp.float32)
        values = mixed[:, :, 2].astype(jnp.float32)
        scores = jnp.einsum('pqhe,pkhe->phqk', query, keys) / math.sqrt(size)
        scores = jnp.where(valid[:, None, None, :], scores, jnp.float32(-1e+30))
        top = lax.optimization_barrier(jnp.max(scores, axis=-1, keepdims=True))
        weights = jnp.exp(scores - top)
        probs = (weights / lax.optimization_barrier(jnp.sum(weights, axis=-1, keepdims=True))).astype(jnp.bfloat16)
        attended = jnp.einsum('phqk,pkhe->pqhe', probs.astype(jnp.float32), values).astype(jnp.bfloat16)
        attended = attended.reshape(count * length, width)
        state = state + jnp.dot(attended, w_out[layer], preferred_element_type=jnp.float32)
        normed = norm_rows(state, layer_gain[layer, 1]).astype(jnp.bfloat16)
        hidden = jax.nn.gelu(jnp.dot(normed, w_up[layer], preferred_element_type=jnp.float32), approximate=True).astype(jnp.bfloat16)
        state = state + jnp.dot(hidden, w_down[layer], preferred_element_type=jnp.float32)
    normed = norm_rows(state, final_gain).astype(jnp.bfloat16)
    intensity = jax.nn.sigmoid(jnp.dot(normed, w_head, preferred_element_type=jnp.float32)).reshape(count, length, -1)
    fragment = jnp.arange(length, dtype=jnp.int32)[None, :] < lengths[:, None] - 1
    intensity = jnp.where(fragment[:, :, None], intensity, jnp.float32(0.0))
    return standardize(intensity.reshape(count, -1))

def best_scores(queries, table, rows, bins):
    blocks = PEPTIDES // PEP_DEV

    def step(carry, block):
        part, part_bins = block
        picked = table[part_bins]
        chosen = queries[picked].astype(jnp.float32)
        scores = jnp.einsum('rqs,rs->rq', chosen, part.astype(jnp.float32)) / math.sqrt(SPEC)
        return (carry.at[picked.reshape(-1)].max(scores.reshape(-1)), None)
    start = jnp.zeros((QUERIES,), jnp.float32)
    result, _ = lax.scan(step, start, (rows.reshape(blocks, PEP_DEV, SPEC), bins.reshape(blocks, PEP_DEV)))
    return result

def reference(peptide_tokens, peptide_lengths, target_owner, target_sub, decoy_owner, decoy_sub, embedding, w_qkv, w_out, w_up, w_down, layer_gain, final_gain, w_head, query_spectra, query_bin):
    blocks = PEPTIDES // PEP_DEV

    def one_block(block):
        tokens, lengths = block
        return predict_block(tokens, lengths, embedding, w_qkv, w_out, w_up, w_down, layer_gain, final_gain, w_head)
    rows = lax.map(one_block, (peptide_tokens.reshape(blocks, PEP_DEV, L), peptide_lengths.reshape(blocks, PEP_DEV)))
    rows = rows.reshape(PEPTIDES, SPEC)
    decoys = rows.reshape(PEPTIDES, L, ION)[:, ::-1, :].reshape(PEPTIDES, SPEC)
    target_bins = (target_owner[:, 0] * BIN_DEV + target_sub).astype(jnp.int32)
    decoy_bins = (decoy_owner[:, 0] * BIN_DEV + decoy_sub).astype(jnp.int32)
    queries = standardize(query_spectra.astype(jnp.float32))
    table = jnp.argsort(query_bin, stable=True).astype(jnp.int32).reshape(BINS, QPB)
    target_best = best_scores(queries, table, rows, target_bins)
    decoy_best = best_scores(queries, table, decoys, decoy_bins)
    return (target_best, decoy_best)
```

```python
import functools
import math

import jax
import jax.numpy as jnp
import numpy as np
from jax import lax
from jax.experimental import pallas as pl
from jax.experimental.pallas import tpu as pltpu
from jax.sharding import PartitionSpec as P

HEADS = 8
L = 32
ION = 32
NL = 2
QPB = 4
D = 256
FF = 1024
SPEC = L * ION
EPS = 1e-06
BF = jnp.bfloat16
F32 = jnp.float32

STEP = 256
TILE = 128
ROWW = SPEC + 128
NT = (((1,), (1,)), ((), ()))
TN = (((0,), (0,)), ((), ()))


def sinusoid():
    place = np.arange(L, dtype=np.float32)[:, None]
    index = np.arange(D // 2, dtype=np.float32)[None, :]
    angle = place * np.exp(-math.log(10000.0) * 2.0 * index / D).astype(np.float32)
    return np.concatenate([np.sin(angle), np.cos(angle)], axis=1).astype(np.float32)


def lane_iota(shape):
    return lax.broadcasted_iota(jnp.int32, shape, len(shape) - 1)


def row_iota(shape):
    return lax.broadcasted_iota(jnp.int32, shape, len(shape) - 2)


def norm_rows(values, gain):
    scale = lax.rsqrt(jnp.mean(values * values, axis=-1, keepdims=True) + EPS)
    return (values * scale * gain).astype(BF)


def standardize(spectra):
    centred = spectra - jnp.mean(spectra, axis=-1, keepdims=True)
    return (centred * lax.rsqrt(jnp.mean(centred * centred, axis=-1, keepdims=True) + EPS)).astype(BF)


def gelu(x):
    inner = x * (math.sqrt(2 / math.pi) + (math.sqrt(2 / math.pi) * 0.044715) * (x * x))
    half = 0.5 * x
    return half + half * jnp.tanh(inner)


def attend(q, k, v, length_lane):
    heads = TILE // L
    lane = lane_iota((TILE, TILE)) // L
    zero = jnp.zeros_like(q)
    spread = jnp.concatenate([jnp.where(lane == h, q, zero) for h in range(heads)], axis=0)
    scores = lax.dot_general(k, spread, NT, preferred_element_type=F32)
    lane4 = (lane_iota((L, heads * TILE)) % TILE) // L
    compact = scores[:L]
    for j in range(1, TILE // L):
        compact = jnp.where(lane4 == j, scores[j * L : (j + 1) * L], compact)
    compact = compact * (1.0 / math.sqrt(L))
    lengths = jnp.concatenate([length_lane] * heads, axis=1)
    compact = jnp.where(row_iota(compact.shape) < lengths, compact, F32(-1e30))
    weights = jnp.exp(compact - jnp.max(compact, axis=0, keepdims=True))
    probs = weights * (1.0 / jnp.sum(weights, axis=0, keepdims=True))
    probs = probs.astype(BF)
    wide = jnp.concatenate(
        [jnp.where(lane4 == j, probs, jnp.zeros_like(probs)) for j in range(TILE // L)], axis=0
    )
    turned = v.T
    out = jnp.concatenate(
        [
            jnp.dot(
                turned[h * L : (h + 1) * L],
                wide[:, h * TILE : (h + 1) * TILE],
                preferred_element_type=F32,
            )
            for h in range(heads)
        ],
        axis=0,
    )
    return out.T.astype(BF)


def predict_kernel(
    lengths_ref,
    tsub_ref,
    dsub_ref,
    tokens_ref,
    towner_ref,
    downer_ref,
    embedding_ref,
    code_ref,
    w_qkv_ref,
    w_out_ref,
    w_up_ref,
    w_down_ref,
    gain_ref,
    final_ref,
    w_head_ref,
    rows_ref,
    logit_ref,
):
    peps = STEP // L
    first = pl.program_id(0) * peps
    tokens = tokens_ref[0]
    onehot = (row_iota((32, STEP)) == tokens).astype(BF)
    state = lax.dot_general(onehot, embedding_ref[...], TN, preferred_element_type=F32)
    state = state + jnp.concatenate([code_ref[...]] * peps, axis=0)

    tile_lengths = []
    for t in range(STEP // TILE):
        lane = lane_iota((1, TILE)) // L
        vec = jnp.full((1, TILE), lengths_ref[first + t * 4], jnp.int32)
        for j in range(1, TILE // L):
            vec = jnp.where(lane == j, lengths_ref[first + t * 4 + j], vec)
        tile_lengths.append(vec)

    for layer in range(NL):
        normed = norm_rows(state, gain_ref[layer, 0:1, :].astype(F32))
        mixed = [
            jnp.dot(
                normed, w_qkv_ref[layer, :, c * D : (c + 1) * D], preferred_element_type=F32
            ).astype(BF)
            for c in range(3)
        ]
        tiles = []
        for t in range(STEP // TILE):
            parts = []
            for g in range(D // TILE):
                q, k, v = [
                    m[t * TILE : (t + 1) * TILE, g * TILE : (g + 1) * TILE] for m in mixed
                ]
                parts.append(attend(q, k, v, tile_lengths[t]))
            tiles.append(jnp.concatenate(parts, axis=1))
        attended = jnp.concatenate(tiles, axis=0)
        state = state + jnp.dot(attended, w_out_ref[layer], preferred_element_type=F32)
        normed = norm_rows(state, gain_ref[layer, 1:2, :].astype(F32))
        for c in range(FF // D):
            up = jnp.dot(
                normed, w_up_ref[layer, :, c * D : (c + 1) * D], preferred_element_type=F32
            )
            hidden = gelu(up).astype(BF)
            state = state + jnp.dot(
                hidden, w_down_ref[layer, c * D : (c + 1) * D, :], preferred_element_type=F32
            )
    normed = norm_rows(state, final_ref[...].astype(F32))
    head = jnp.concatenate([w_head_ref[...]] * 4, axis=1)
    logit_ref[...] = jnp.dot(normed, head, preferred_element_type=F32)

    lane = lane_iota((peps, 128)) // ION
    tiles = []
    for t in range(SPEC // 128):
        tile = logit_ref[pl.ds(4 * t, peps, stride=L), :]
        for i in range(1, 4):
            tile = jnp.where(lane == i, logit_ref[pl.ds(4 * t + i, peps, stride=L), :], tile)
        tiles.append(tile)
    logits = jnp.concatenate(tiles, axis=1)
    intensity = 1.0 / (1.0 + jnp.exp(-logits))
    where_row = row_iota((peps, 128))
    length = jnp.zeros((peps, 128), jnp.int32)
    tsub = jnp.zeros((peps, 128), jnp.int32)
    dsub = jnp.zeros((peps, 128), jnp.int32)
    for i in range(peps):
        length = jnp.where(where_row == i, lengths_ref[first + i], length)
        tsub = jnp.where(where_row == i, tsub_ref[first + i], tsub)
        dsub = jnp.where(where_row == i, dsub_ref[first + i], dsub)
    position = lane_iota((peps, SPEC)) // ION
    length = jnp.concatenate([length] * (SPEC // 128), axis=1)
    intensity = jnp.where(position < length - 1, intensity, F32(0.0))
    start = pl.multiple_of(first, peps)
    rows_ref[:, :SPEC] = standardize(intensity)
    column = lane_iota((peps, 128))
    tag = jnp.where(column == 0, towner_ref[...], tsub)
    tag = jnp.where(column == 2, downer_ref[...], tag)
    tag = jnp.where(column == 3, dsub, tag)
    rows_ref[:, SPEC:] = tag.astype(F32).astype(BF)


def predict_rows(
    tokens, lengths, towner, tsub, downer, dsub, embedding, w_qkv, w_out, w_up, w_down, gains, final, w_head
):
    count = tokens.shape[0]
    peps = STEP // L
    steps = count // peps
    whole = lambda shape: pl.BlockSpec(shape, lambda i, *_: (0,) * len(shape))
    grid = pltpu.PrefetchScalarGridSpec(
        num_scalar_prefetch=3,
        grid=(steps,),
        in_specs=[
            pl.BlockSpec((1, 1, STEP), lambda i, *_: (i, 0, 0)),
            pl.BlockSpec((peps, 1), lambda i, *_: (i, 0)),
            pl.BlockSpec((peps, 1), lambda i, *_: (i, 0)),
            whole(embedding.shape),
            whole((L, D)),
            whole(w_qkv.shape),
            whole(w_out.shape),
            whole(w_up.shape),
            whole(w_down.shape),
            whole(gains.shape),
            whole((1, D)),
            whole(w_head.shape),
        ],
        out_specs=pl.BlockSpec((peps, ROWW), lambda i, *_: (i, 0)),
        scratch_shapes=[pltpu.VMEM((STEP, 128), F32)],
    )
    return pl.pallas_call(
        predict_kernel,
        grid_spec=grid,
        out_shape=jax.ShapeDtypeStruct((count, ROWW), BF),
        compiler_params=pltpu.CompilerParams(vmem_limit_bytes=40 * 1024 * 1024),
        name="predict",
    )(
        lengths,
        tsub,
        dsub,
        tokens.reshape(steps, 1, STEP),
        towner,
        downer,
        embedding,
        jnp.asarray(sinusoid()),
        w_qkv,
        w_out,
        w_up,
        w_down,
        gains,
        final.reshape(1, D),
        w_head,
    )


def slots_of(bins):
    count = bins.shape[1]
    across = jnp.broadcast_to(bins.astype(F32), (count, count))
    down = across.T
    earlier = (across == down) & (row_iota((count, count)) < lane_iota((count, count)))
    rank = jnp.sum(earlier.astype(F32), axis=0, keepdims=True)
    local = bins.astype(F32) - jnp.min(bins.astype(F32), axis=1, keepdims=True)
    return (local * QPB + rank).astype(jnp.int32)


def query_kernel(bins_ref, spectra_ref, out_ref):
    count = spectra_ref.shape[0]
    place = (row_iota((count, count)) == slots_of(bins_ref[...])).astype(BF)
    ready = standardize(spectra_ref[...].astype(F32))
    out_ref[...] = jnp.dot(place, ready, preferred_element_type=F32).astype(BF)


def prepare_queries(query_bin, spectra):
    count = spectra.shape[0]
    return pl.pallas_call(
        query_kernel,
        out_shape=jax.ShapeDtypeStruct(spectra.shape, BF),
        name="prepare",
    )(query_bin.reshape(1, count), spectra)


QBLOCK = 256


def score_kernel(me_ref, queries_ref, *refs):
    sources, out_ref = refs[:-1], refs[-1]
    rows = jnp.concatenate([ref[:, :SPEC] for ref in sources], axis=0)
    tags = jnp.concatenate([ref[:, SPEC:] for ref in sources], axis=0).astype(F32)
    queries = queries_ref[...]
    turn = (
        row_iota((128, 128)) // ION * ION + lane_iota((128, 128)) % ION
        == (3 - lane_iota((128, 128)) // ION) * ION + lane_iota((128, 128)) % ION
    ) & (row_iota((128, 128)) % ION == lane_iota((128, 128)) % ION)
    turn = turn.astype(BF)
    tiles = SPEC // 128
    turned = jnp.concatenate(
        [
            jnp.dot(
                queries[:, (tiles - 1 - t) * 128 : (tiles - t) * 128], turn, preferred_element_type=F32
            ).astype(BF)
            for t in range(tiles)
        ],
        axis=1,
    )
    me = me_ref[0].astype(F32)
    first = pl.program_id(0) * (QBLOCK // QPB)
    bins = (lane_iota((1, QBLOCK)) // QPB + first).astype(F32)
    best = []
    for kind, side in enumerate((queries, turned)):
        scores = lax.dot_general(rows, side, NT, preferred_element_type=F32)
        sub = jnp.where(tags[:, 2 * kind : 2 * kind + 1] == me, tags[:, 2 * kind + 1 : 2 * kind + 2], F32(-1.0))
        scores = jnp.where(sub == bins, scores, F32(0.0))
        best.append(jnp.max(scores, axis=0, keepdims=True) * F32(1.0 / math.sqrt(SPEC)))
    lane = lane_iota((8, 128))
    row = row_iota((8, 128))
    out = jnp.zeros((8, 128), F32)
    for s in range(QBLOCK // 32):
        tile, shift = s // 4, 32 * (s % 4)
        pair = [jnp.broadcast_to(b[:, tile * 128 : (tile + 1) * 128], (8, 128)) for b in best]
        near = pltpu.roll(pair[0], (128 - shift) % 128, 1)
        far = pltpu.roll(pair[1], (128 - shift + 32) % 128, 1)
        out = jnp.where(row == s, jnp.where(lane < 32, near, far), out)
    out_ref[...] = out


def score(me, queries, sources):
    blocks = queries.shape[0] // QBLOCK
    count = sources[0].shape[0]
    return pl.pallas_call(
        score_kernel,
        grid=(blocks,),
        in_specs=[
            pl.BlockSpec(memory_space=pltpu.SMEM),
            pl.BlockSpec((QBLOCK, SPEC), lambda i: (i, 0)),
        ]
        + [pl.BlockSpec((count, ROWW), lambda i: (0, 0))] * len(sources),
        out_specs=pl.BlockSpec((QBLOCK // 32, 128), lambda i: (i, 0)),
        out_shape=jax.ShapeDtypeStruct((queries.shape[0] // 32, 128), F32),
        compiler_params=pltpu.CompilerParams(vmem_limit_bytes=40 * 1024 * 1024),
        name="score",
    )(me, queries, *sources)


def finish_kernel(bins_ref, pieces_ref, target_ref, decoy_ref):
    count = bins_ref.shape[1]
    best = jnp.maximum(jnp.max(pieces_ref[...], axis=0, keepdims=True), F32(0.0))
    slots = slots_of(bins_ref[...])
    place = row_iota((count, count)) == slots
    for kind, ref in enumerate((target_ref, decoy_ref)):
        wide = jnp.broadcast_to(best[:, kind * count : (kind + 1) * count], (count, count)).T
        ref[...] = jnp.sum(jnp.where(place, wide, F32(0.0)), axis=0, keepdims=True)


def finish(query_bin, pieces):
    count = query_bin.shape[0]
    shape = jax.ShapeDtypeStruct((1, count), F32)
    target, decoy = pl.pallas_call(finish_kernel, out_shape=(shape, shape), name="finish")(
        query_bin.reshape(1, count), pieces
    )
    return target.reshape(count), decoy.reshape(count)


def local(
    xs,
    ys,
    zs,
    peptide_tokens,
    peptide_lengths,
    target_owner,
    target_sub,
    decoy_owner,
    decoy_sub,
    embedding,
    w_qkv,
    w_out,
    w_up,
    w_down,
    layer_gain,
    final_gain,
    w_head,
    query_spectra,
    query_bin,
):
    along_z = [[y * zs + z for z in range(zs)] for y in range(ys)]
    along_y = [[y * zs + z for y in range(ys)] for z in range(zs)]
    queries = prepare_queries(query_bin, query_spectra)
    queries = lax.all_gather(queries, "seq", axis=0, tiled=True, axis_index_groups=along_z)
    queries = lax.all_gather(queries, "seq", axis=0, tiled=True, axis_index_groups=along_y)
    rows = predict_rows(
        peptide_tokens,
        peptide_lengths,
        target_owner,
        target_sub,
        decoy_owner,
        decoy_sub,
        embedding,
        w_qkv,
        w_out,
        w_up,
        w_down,
        layer_gain,
        final_gain,
        w_head,
    )
    swap = [(i, i ^ 1) for i in range(2 * xs)]
    held = [rows] + [
        lax.ppermute(rows, "mass", [(i, (i + 2 * d) % (2 * xs)) for i in range(2 * xs)])
        for d in range(1, xs)
    ]
    held = held + [lax.ppermute(part, "mass", swap) for part in held]
    me = lax.axis_index("mass").astype(jnp.int32).reshape(1)
    pieces = score(me, queries, held)
    pieces = lax.all_to_all(pieces, "seq", split_axis=0, concat_axis=0, tiled=True)
    return finish(query_bin, pieces)


def solution(mesh):
    in_specs = (
        P(("mass", "seq"), None),
        P(("mass", "seq")),
        P(("mass", "seq"), None),
        P(("mass", "seq")),
        P(("mass", "seq"), None),
        P(("mass", "seq")),
        P(),
        P(),
        P(),
        P(),
        P(),
        P(),
        P(),
        P(),
        P(("mass", "seq"), None),
        P(("mass", "seq")),
    )
    out_specs = (P(("mass", "seq")), P(("mass", "seq")))
    body = functools.partial(local, mesh.shape["mass"] // 2, 4, mesh.shape["seq"] // 4)
    return jax.shard_map(body, mesh=mesh, in_specs=in_specs, out_specs=out_specs, check_vma=False)
```

```python
import functools
import math

import jax
import jax.numpy as jnp
import numpy as np
from jax import lax
from jax.experimental import pallas as pl
from jax.experimental.pallas import tpu as pltpu
from jax.sharding import PartitionSpec as P

HEADS = 8
L = 32
ION = 32
NL = 2
QPB = 4
D = 256
FF = 1024
SPEC = L * ION
EPS = 1e-06
BF = jnp.bfloat16
F32 = jnp.float32

STEP = 1024
TILE = 128
GROUP = 8
ROWW = SPEC + 128
VMEM_LIMIT = 60 * 1024 * 1024
NT = (((1,), (1,)), ((), ()))


def sinusoid():
    place = np.arange(L, dtype=np.float32)[:, None]
    index = np.arange(D // 2, dtype=np.float32)[None, :]
    angle = place * np.exp(-math.log(10000.0) * 2.0 * index / D).astype(np.float32)
    return np.concatenate([np.sin(angle), np.cos(angle)], axis=1).astype(np.float32)


def lane_iota(shape):
    return lax.broadcasted_iota(jnp.int32, shape, len(shape) - 1)


def row_iota(shape):
    return lax.broadcasted_iota(jnp.int32, shape, len(shape) - 2)


def norm_rows(values, gain):
    scale = lax.rsqrt(jnp.mean(values * values, axis=-1, keepdims=True) + EPS)
    return (values * scale * gain).astype(BF)


def standardize(spectra):
    centred = spectra - jnp.mean(spectra, axis=-1, keepdims=True)
    return (centred * lax.rsqrt(jnp.mean(centred * centred, axis=-1, keepdims=True) + EPS)).astype(BF)


def gelu(x):
    inner = x * (math.sqrt(2 / math.pi) + (math.sqrt(2 / math.pi) * 0.044715) * (x * x))
    half = 0.5 * x
    return half + half * jnp.tanh(inner)


def feed_forward(state, normed, w_up_ref, w_down_ref):
    hidden = gelu(jnp.dot(normed, w_up_ref[...], preferred_element_type=F32)).astype(BF)
    return state + jnp.dot(hidden, w_down_ref[...], preferred_element_type=F32)


def attend(items):
    heads, peps = TILE // L, TILE // L
    lane = (lane_iota((L, heads * TILE)) % TILE) // L
    empty = jnp.zeros((L, TILE), BF)
    scores = []
    for query, key, _, _ in items:
        turned = query.T
        spread = [
            jnp.concatenate(
                [turned[h * L : (h + 1) * L] if h == i else empty for i in range(heads)], axis=1
            )
            for h in range(heads)
        ]
        spread = jnp.concatenate(spread, axis=0)
        scores.append(jnp.dot(key, spread, preferred_element_type=F32))
    wide = []
    for score, (_, _, _, length) in zip(scores, items):
        own = score[:L]
        for j in range(1, peps):
            own = jnp.where(lane == j, score[j * L : (j + 1) * L], own)
        own = own * (1.0 / math.sqrt(L))
        own = jnp.where(
            row_iota(own.shape) < jnp.concatenate([length] * heads, axis=1), own, F32(-1e30)
        )
        weights = jnp.exp(own - jnp.max(own, axis=0, keepdims=True))
        probs = weights * (1.0 / jnp.sum(weights, axis=0, keepdims=True))
        probs = probs.astype(BF)
        wide.append(
            jnp.concatenate(
                [jnp.where(lane == j, probs, jnp.zeros_like(probs)) for j in range(peps)], axis=0
            )
        )
    heard = []
    for probs, (_, _, value, _) in zip(wide, items):
        turned = value.T
        heard.append(
            jnp.concatenate(
                [
                    jnp.dot(
                        turned[h * L : (h + 1) * L],
                        probs[:, h * TILE : (h + 1) * TILE],
                        preferred_element_type=F32,
                    )
                    for h in range(heads)
                ],
                axis=0,
            )
        )
    return [out.T.astype(BF) for out in heard]


def predict_kernel(
    lengths_ref,
    towner_ref,
    tsub_ref,
    downer_ref,
    dsub_ref,
    tokens_ref,
    embedding_ref,
    code_ref,
    w_qkv_ref,
    w_out_ref,
    w_up_ref,
    w_down_ref,
    gain_ref,
    final_ref,
    w_head_ref,
    rows_ref,
    logit_ref,
):
    peps = STEP // L
    first = pl.program_id(0) * peps
    tokens = tokens_ref[...]
    tokens = jnp.concatenate([tokens] * (128 // tokens.shape[1]), axis=1)
    tokens = pltpu.roll(tokens, 128 - first, 1)
    vocab = embedding_ref.shape[0]
    onehot = jnp.concatenate(
        [tokens[:, j : j + 1] == lane_iota((L, vocab)) for j in range(peps)], axis=0
    ).astype(BF)
    state = jnp.dot(onehot, embedding_ref[...], preferred_element_type=F32)
    state = state + jnp.concatenate([code_ref[...]] * peps, axis=0)

    tile_lengths = []
    for t in range(STEP // TILE):
        lane = lane_iota((1, TILE)) // L
        vec = jnp.full((1, TILE), lengths_ref[first + t * 4], jnp.int32)
        for j in range(1, TILE // L):
            vec = jnp.where(lane == j, lengths_ref[first + t * 4 + j], vec)
        tile_lengths.append(vec)

    for layer in range(NL):
        normed = norm_rows(state, gain_ref[layer, 0:1, :].astype(F32))
        mixed = [
            jnp.dot(
                normed, w_qkv_ref[layer, :, c * D : (c + 1) * D], preferred_element_type=F32
            ).astype(BF)
            for c in range(3)
        ]
        items = [
            [m[t * TILE : (t + 1) * TILE, g * TILE : (g + 1) * TILE] for m in mixed] + [tile_lengths[t]]
            for t in range(STEP // TILE)
            for g in range(D // TILE)
        ]
        heard = []
        for i in range(0, len(items), GROUP):
            heard = heard + attend(items[i : i + GROUP])
        attended = jnp.concatenate(
            [jnp.concatenate(heard[i : i + 2], axis=1) for i in range(0, len(heard), 2)], axis=0
        )
        state = state + jnp.dot(attended, w_out_ref[layer], preferred_element_type=F32)
        normed = norm_rows(state, gain_ref[layer, 1:2, :].astype(F32))
        state = feed_forward(state, normed, w_up_ref.at[layer], w_down_ref.at[layer])
    normed = norm_rows(state, final_ref[...].reshape(1, D).astype(F32))
    head = jnp.concatenate([w_head_ref[...]] * 4, axis=0)
    logit_ref[...] = lax.dot_general(normed, head, NT, preferred_element_type=F32)

    lane = lane_iota((peps, 128)) // ION
    tiles = []
    for t in range(SPEC // 128):
        tile = logit_ref[pl.ds(4 * t, peps, stride=L), :]
        for i in range(1, 4):
            tile = jnp.where(lane == i, logit_ref[pl.ds(4 * t + i, peps, stride=L), :], tile)
        tiles.append(tile)
    logits = jnp.concatenate(tiles, axis=1)
    intensity = 1.0 / (1.0 + jnp.exp(-logits))
    row = row_iota((peps, 128))
    column = lane_iota((peps, 128))
    length = jnp.zeros((peps, 128), jnp.int32)
    tag = jnp.zeros((peps, 128), jnp.int32)
    for i in range(peps):
        length = jnp.where(row == i, lengths_ref[first + i], length)
        for c, ref in enumerate((towner_ref, tsub_ref, downer_ref, dsub_ref)):
            tag = jnp.where((row == i) & (column == c), ref[first + i], tag)
    position = lane_iota((peps, SPEC)) // ION
    length = jnp.concatenate([length] * (SPEC // 128), axis=1)
    intensity = jnp.where(position < length - 1, intensity, F32(0.0))
    rows_ref[:, :SPEC] = standardize(intensity)
    rows_ref[:, SPEC:] = tag.astype(F32).astype(BF)


def predict_rows(
    tokens, lengths, towner, tsub, downer, dsub, embedding, w_qkv, w_out, w_up, w_down, gains, final, w_head
):
    count = tokens.shape[0]
    peps = STEP // L
    steps = count // peps
    whole = lambda shape: pl.BlockSpec(shape, lambda i, *_: (0,) * len(shape))
    operands = (
        tokens.T,
        embedding,
        jnp.asarray(sinusoid()),
        w_qkv,
        w_out,
        w_up,
        w_down,
        gains,
        final,
        w_head.T,
    )
    grid = pltpu.PrefetchScalarGridSpec(
        num_scalar_prefetch=5,
        grid=(steps,),
        in_specs=[whole(operand.shape) for operand in operands],
        out_specs=pl.BlockSpec((peps, ROWW), lambda i, *_: (i, 0)),
        scratch_shapes=[pltpu.VMEM((STEP, 128), F32)],
    )
    return pl.pallas_call(
        predict_kernel,
        grid_spec=grid,
        out_shape=jax.ShapeDtypeStruct((count, ROWW), BF),
        compiler_params=pltpu.CompilerParams(vmem_limit_bytes=VMEM_LIMIT),
        name="predict",
    )(lengths, towner.reshape(count), tsub, downer.reshape(count), dsub, *operands)


def slots_of(bins):
    count = bins.shape[1]
    across = jnp.broadcast_to(bins.astype(F32), (count, count))
    down = across.T
    earlier = (across == down) & (row_iota((count, count)) < lane_iota((count, count)))
    rank = jnp.sum(earlier.astype(F32), axis=0, keepdims=True)
    local = bins.astype(F32) - jnp.min(bins.astype(F32), axis=1, keepdims=True)
    return (local * QPB + rank).astype(jnp.int32)


def query_kernel(bins_ref, spectra_ref, out_ref):
    count = spectra_ref.shape[0]
    place = (row_iota((count, count)) == slots_of(bins_ref[...])).astype(BF)
    ready = standardize(spectra_ref[...].astype(F32))
    out_ref[...] = jnp.dot(place, ready, preferred_element_type=F32).astype(BF)


def prepare_queries(query_bin, spectra):
    count = spectra.shape[0]
    return pl.pallas_call(
        query_kernel,
        out_shape=jax.ShapeDtypeStruct(spectra.shape, BF),
        compiler_params=pltpu.CompilerParams(vmem_limit_bytes=VMEM_LIMIT),
        name="prepare",
    )(query_bin.reshape(1, count), spectra)


QBLOCK = 256


def score_kernel(ys, zs, mass_ref, seq_ref, queries_ref, *refs):
    sources, out_ref, held_ref, sems = refs[:-3], refs[-3], refs[-2], refs[-1]
    blocks = queries_ref.shape[0] // QBLOCK
    copies = [
        pltpu.make_async_copy(
            queries_ref.at[pl.ds(i * QBLOCK, QBLOCK)], held_ref.at[pl.ds(i * QBLOCK, QBLOCK)], sems.at[i]
        )
        for i in range(blocks)
    ]
    for copy in copies:
        copy.start()
    rows = jnp.concatenate([ref[:, :SPEC] for ref in sources], axis=0)
    tags = jnp.concatenate([ref[:, SPEC:] for ref in sources], axis=0).astype(F32)
    me, y = mass_ref[0].astype(F32), lax.div(seq_ref[0], zs)
    subs = []
    for kind in range(2):
        owner, sub = tags[:, 2 * kind : 2 * kind + 1], tags[:, 2 * kind + 1 : 2 * kind + 2]
        subs.append(jnp.where(owner == me, sub, F32(-1.0)))
    row, lane = row_iota((128, 128)), lane_iota((128, 128))
    turn = ((row // ION == 3 - lane // ION) & (row % ION == lane % ION)).astype(BF)
    tiles = SPEC // 128
    lane = lane_iota((1, QBLOCK))
    low = lane_iota((8, 128)) < 32
    for block, copy in enumerate(copies):
        copy.wait()
        queries = held_ref[block * QBLOCK : (block + 1) * QBLOCK, :]
        turned = jnp.concatenate(
            [
                jnp.dot(
                    queries[:, (tiles - 1 - t) * 128 : (tiles - t) * 128], turn, preferred_element_type=F32
                ).astype(BF)
                for t in range(tiles)
            ],
            axis=1,
        )
        z = lane // 128 + block * (QBLOCK // 128)
        bins = (lax.rem(y + ys - lane % 128 // 32, ys) * zs + z) * (32 // QPB) + lane % 32 // QPB
        bins = bins.astype(F32)
        best = []
        for sub, side in zip(subs, (queries, turned)):
            scores = lax.dot_general(rows, side, NT, preferred_element_type=F32)
            scores = jnp.where(sub == bins, scores, F32(0.0))
            best.append(jnp.max(scores, axis=0, keepdims=True) * F32(1.0 / math.sqrt(SPEC)))
        for s in range(QBLOCK // 32):
            tile, back = s // 4, s % 4
            pair = [jnp.broadcast_to(b[:, tile * 128 : (tile + 1) * 128], (8, 128)) for b in best]
            near = pltpu.roll(pair[0], (128 - 32 * back) % 128, 1)
            far = pltpu.roll(pair[1], (128 - 32 * back + 32) % 128, 1)
            z = block * (QBLOCK // 128) + tile
            out_ref[pl.ds(lax.rem(y + ys - back, ys) * zs + z, 1), :] = jnp.where(low, near, far)[:1]


def score(ys, zs, mass, seq, queries, sources):
    spot = pl.BlockSpec(memory_space=pltpu.SMEM)
    return pl.pallas_call(
        functools.partial(score_kernel, ys, zs),
        in_specs=[spot, spot, pl.BlockSpec(memory_space=pltpu.HBM)]
        + [pl.BlockSpec(memory_space=pltpu.VMEM)] * len(sources),
        out_specs=pl.BlockSpec(memory_space=pltpu.VMEM),
        out_shape=jax.ShapeDtypeStruct((queries.shape[0] // 32, 128), F32),
        scratch_shapes=[
            pltpu.VMEM(queries.shape, BF),
            pltpu.SemaphoreType.DMA((queries.shape[0] // QBLOCK,)),
        ],
        compiler_params=pltpu.CompilerParams(vmem_limit_bytes=62 * 1024 * 1024),
        name="score",
    )(mass, seq, queries, *sources)


def finish_kernel(bins_ref, pieces_ref, target_ref, decoy_ref):
    count = bins_ref.shape[1]
    best = jnp.maximum(jnp.max(pieces_ref[...], axis=0, keepdims=True), F32(0.0))
    slots = slots_of(bins_ref[...])
    place = row_iota((count, count)) == slots
    for kind, ref in enumerate((target_ref, decoy_ref)):
        wide = jnp.broadcast_to(best[:, kind * count : (kind + 1) * count], (count, count)).T
        ref[...] = jnp.sum(jnp.where(place, wide, F32(0.0)), axis=0, keepdims=True)


def finish(query_bin, pieces):
    count = query_bin.shape[0]
    shape = jax.ShapeDtypeStruct((1, count), F32)
    target, decoy = pl.pallas_call(finish_kernel, out_shape=(shape, shape), name="finish")(
        query_bin.reshape(1, count), pieces
    )
    return target.reshape(count), decoy.reshape(count)


def local(
    xs,
    ys,
    zs,
    peptide_tokens,
    peptide_lengths,
    target_owner,
    target_sub,
    decoy_owner,
    decoy_sub,
    embedding,
    w_qkv,
    w_out,
    w_up,
    w_down,
    layer_gain,
    final_gain,
    w_head,
    query_spectra,
    query_bin,
):
    along_z = [[y * zs + z for z in range(zs)] for y in range(ys)]
    queries = prepare_queries(query_bin, query_spectra)
    queries = [queries] + [
        lax.ppermute(queries, "seq", [(i, (i + d * zs) % (ys * zs)) for i in range(ys * zs)])
        for d in range(1, ys)
    ]
    queries = lax.all_gather(
        jnp.concatenate(queries, axis=0), "seq", axis=0, tiled=True, axis_index_groups=along_z
    )
    rows = predict_rows(
        peptide_tokens,
        peptide_lengths,
        target_owner,
        target_sub,
        decoy_owner,
        decoy_sub,
        embedding,
        w_qkv,
        w_out,
        w_up,
        w_down,
        layer_gain,
        final_gain,
        w_head,
    )
    swap = [(i, i ^ 1) for i in range(2 * xs)]
    held = [rows] + [
        lax.ppermute(rows, "mass", [(i, (i + 2 * d) % (2 * xs)) for i in range(2 * xs)])
        for d in range(1, xs)
    ]
    held = held + [lax.ppermute(part, "mass", swap) for part in held]
    mass, seq = [lax.axis_index(axis).astype(jnp.int32).reshape(1) for axis in ("mass", "seq")]
    pieces = score(ys, zs, mass, seq, queries, held)[:, None, :]
    pieces = lax.all_to_all(pieces, "seq", split_axis=0, concat_axis=0, tiled=True)[:, 0, :]
    return finish(query_bin, pieces)


def solution(mesh):
    in_specs = (
        P(("mass", "seq"), None),
        P(("mass", "seq")),
        P(("mass", "seq"), None),
        P(("mass", "seq")),
        P(("mass", "seq"), None),
        P(("mass", "seq")),
        P(),
        P(),
        P(),
        P(),
        P(),
        P(),
        P(),
        P(),
        P(("mass", "seq"), None),
        P(("mass", "seq")),
    )
    out_specs = (P(("mass", "seq")), P(("mass", "seq")))
    body = functools.partial(local, mesh.shape["mass"] // 2, 4, mesh.shape["seq"] // 4)
    return jax.shard_map(body, mesh=mesh, in_specs=in_specs, out_specs=out_specs, check_vma=False)
```

```python
import functools
import math

import jax
import jax.numpy as jnp
import numpy as np
from jax import lax
from jax.experimental import pallas as pl
from jax.experimental.pallas import tpu as pltpu
from jax.sharding import PartitionSpec as P

HEADS = 8
L = 32
ION = 32
NL = 2
QPB = 4
YS = 4
D = 256
FF = 1024
SPEC = L * ION
EPS = 1e-06
BF = jnp.bfloat16
F32 = jnp.float32

STEP = 1024
TILE = 128
GROUP = 8
PIECES = 1
ROWW = SPEC + 128
VMEM_LIMIT = 60 * 1024 * 1024
NT = (((1,), (1,)), ((), ()))


def sinusoid():
    place = np.arange(L, dtype=np.float32)[:, None]
    index = np.arange(D // 2, dtype=np.float32)[None, :]
    angle = place * np.exp(-math.log(10000.0) * 2.0 * index / D).astype(np.float32)
    return np.concatenate([np.sin(angle), np.cos(angle)], axis=1).astype(np.float32)


def lane_iota(shape):
    return lax.broadcasted_iota(jnp.int32, shape, len(shape) - 1)


def row_iota(shape):
    return lax.broadcasted_iota(jnp.int32, shape, len(shape) - 2)


def norm_rows(values, gain):
    scale = lax.rsqrt(jnp.mean(values * values, axis=-1, keepdims=True) + EPS)
    return (values * scale * gain).astype(BF)


def standardize(spectra):
    centred = spectra - jnp.mean(spectra, axis=-1, keepdims=True)
    return (centred * lax.rsqrt(jnp.mean(centred * centred, axis=-1, keepdims=True) + EPS)).astype(BF)


def gelu(x):
    inner = x * (math.sqrt(2 / math.pi) + (math.sqrt(2 / math.pi) * 0.044715) * (x * x))
    half = 0.5 * x
    return half + half * jnp.tanh(inner)


def feed_forward(state, normed, w_up_ref, w_down_ref):
    for c in range(0, FF, D):
        up = jnp.dot(normed, w_up_ref[:, c : c + D], preferred_element_type=F32)
        hidden = gelu(up).astype(BF)
        state = state + jnp.dot(hidden, w_down_ref[c : c + D, :], preferred_element_type=F32)
    return state


def attend(items):
    heads, peps = TILE // L, TILE // L
    lane = (lane_iota((L, heads * TILE)) % TILE) // L
    empty = jnp.zeros((L, TILE), BF)
    scores = []
    for query, key, _, _ in items:
        turned = query.T
        spread = [
            jnp.concatenate(
                [turned[h * L : (h + 1) * L] if h == i else empty for i in range(heads)], axis=1
            )
            for h in range(heads)
        ]
        spread = jnp.concatenate(spread, axis=0)
        scores.append(jnp.dot(key, spread, preferred_element_type=F32))
    wide = []
    for score, (_, _, _, length) in zip(scores, items):
        own = score[:L]
        for j in range(1, peps):
            own = jnp.where(lane == j, score[j * L : (j + 1) * L], own)
        own = own * (1.0 / math.sqrt(L))
        own = jnp.where(
            row_iota(own.shape) < jnp.concatenate([length] * heads, axis=1), own, F32(-1e30)
        )
        weights = jnp.exp(own - jnp.max(own, axis=0, keepdims=True))
        probs = weights * (1.0 / jnp.sum(weights, axis=0, keepdims=True))
        probs = probs.astype(BF)
        wide.append(
            jnp.concatenate(
                [jnp.where(lane == j, probs, jnp.zeros_like(probs)) for j in range(peps)], axis=0
            )
        )
    heard = []
    for probs, (_, _, value, _) in zip(wide, items):
        turned = value.T
        heard.append(
            jnp.concatenate(
                [
                    jnp.dot(
                        turned[h * L : (h + 1) * L],
                        probs[:, h * TILE : (h + 1) * TILE],
                        preferred_element_type=F32,
                    )
                    for h in range(heads)
                ],
                axis=0,
            )
        )
    return [out.T.astype(BF) for out in heard]


def predict_kernel(
    base,
    lengths_ref,
    towner_ref,
    tsub_ref,
    downer_ref,
    dsub_ref,
    tokens_ref,
    embedding_ref,
    code_ref,
    w_qkv_ref,
    w_out_ref,
    w_up_ref,
    w_down_ref,
    gain_ref,
    final_ref,
    w_head_ref,
    *refs,
):
    rows_ref, logit_ref, sems = refs[-7], refs[-6], refs[-1]
    peps = STEP // L
    sources = (w_qkv_ref, w_out_ref, w_up_ref, w_down_ref)
    kept = refs[-5:-1]
    moves = [
        [
            pltpu.make_async_copy(
                source.at[layer, pl.ds(p * source.shape[1] // PIECES, source.shape[1] // PIECES)],
                held.at[layer, pl.ds(p * source.shape[1] // PIECES, source.shape[1] // PIECES)],
                sems.at[layer, i, p],
            )
            for i, (source, held) in enumerate(zip(sources, kept))
            for p in range(PIECES)
        ]
        for layer in range(NL)
    ]
    w_qkv_ref, w_out_ref, w_up_ref, w_down_ref = kept
    for move in moves[0] + moves[1]:
        move.start()

    first = base
    tokens = tokens_ref[...]
    tokens = jnp.concatenate([tokens] * (128 // tokens.shape[1]), axis=1)
    tokens = pltpu.roll(tokens, (128 - first) % 128, 1)
    vocab = embedding_ref.shape[0]
    onehot = jnp.concatenate(
        [tokens[:, j : j + 1] == lane_iota((L, vocab)) for j in range(peps)], axis=0
    ).astype(BF)
    state = jnp.dot(onehot, embedding_ref[...], preferred_element_type=F32)
    state = state + jnp.concatenate([code_ref[...]] * peps, axis=0)

    tile_lengths = []
    for t in range(STEP // TILE):
        lane = lane_iota((1, TILE)) // L
        vec = jnp.full((1, TILE), lengths_ref[first + t * 4], jnp.int32)
        for j in range(1, TILE // L):
            vec = jnp.where(lane == j, lengths_ref[first + t * 4 + j], vec)
        tile_lengths.append(vec)

    for layer in range(NL):
        normed = norm_rows(state, gain_ref[layer, 0:1, :].astype(F32))
        for move in moves[layer]:
            move.wait()
        mixed = [
            jnp.dot(
                normed, w_qkv_ref[layer, :, c * D : (c + 1) * D], preferred_element_type=F32
            ).astype(BF)
            for c in range(3)
        ]
        items = [
            [m[t * TILE : (t + 1) * TILE, g * TILE : (g + 1) * TILE] for m in mixed] + [tile_lengths[t]]
            for t in range(STEP // TILE)
            for g in range(D // TILE)
        ]
        heard = []
        for i in range(0, len(items), GROUP):
            heard = heard + attend(items[i : i + GROUP])
        attended = jnp.concatenate(
            [jnp.concatenate(heard[i : i + 2], axis=1) for i in range(0, len(heard), 2)], axis=0
        )
        state = state + jnp.dot(attended, w_out_ref[layer], preferred_element_type=F32)
        normed = norm_rows(state, gain_ref[layer, 1:2, :].astype(F32))
        state = feed_forward(state, normed, w_up_ref.at[layer], w_down_ref.at[layer])
    normed = norm_rows(state, final_ref[...].reshape(1, D).astype(F32))
    head = jnp.concatenate([w_head_ref[...]] * 4, axis=0)
    logit_ref[...] = lax.dot_general(normed, head, NT, preferred_element_type=F32)

    lane = lane_iota((peps, 128)) // ION
    tiles = []
    for t in range(SPEC // 128):
        tile = logit_ref[pl.ds(4 * t, peps, stride=L), :]
        for i in range(1, 4):
            tile = jnp.where(lane == i, logit_ref[pl.ds(4 * t + i, peps, stride=L), :], tile)
        tiles.append(tile)
    logits = jnp.concatenate(tiles, axis=1)
    intensity = 1.0 / (1.0 + jnp.exp(-logits))
    row = row_iota((peps, 128))
    column = lane_iota((peps, 128))
    length = jnp.zeros((peps, 128), jnp.int32)
    tag = jnp.zeros((peps, 128), jnp.int32)
    for i in range(peps):
        length = jnp.where(row == i, lengths_ref[first + i], length)
        for c, ref in enumerate((towner_ref, tsub_ref, downer_ref, dsub_ref)):
            tag = jnp.where((row == i) & (column == c), ref[first + i], tag)
    position = lane_iota((peps, SPEC)) // ION
    length = jnp.concatenate([length] * (SPEC // 128), axis=1)
    intensity = jnp.where(position < length - 1, intensity, F32(0.0))
    rows_ref[:, :SPEC] = standardize(intensity)
    rows_ref[:, SPEC:] = tag.astype(F32).astype(BF)


def predict_rows(
    part,
    parts,
    before,
    tokens,
    lengths,
    towner,
    tsub,
    downer,
    dsub,
    embedding,
    w_qkv,
    w_out,
    w_up,
    w_down,
    gains,
    final,
    w_head,
):
    count = tokens.shape[0]
    peps = STEP // L
    assert parts * peps == count
    whole = lambda shape: pl.BlockSpec(shape, lambda i, *_: (0,) * len(shape))
    operands = (
        tokens.T,
        embedding,
        jnp.asarray(sinusoid()),
        w_qkv,
        w_out,
        w_up,
        w_down,
        gains,
        final,
        w_head.T,
    )
    large = (w_qkv, w_out, w_up, w_down)
    in_specs = [
        pl.BlockSpec(memory_space=pltpu.HBM) if operand.ndim == 3 and operand is not gains else whole(operand.shape)
        for operand in operands
    ]
    scalars = (lengths, towner.reshape(count), tsub, downer.reshape(count), dsub)
    aliases = {}
    if before is not None:
        aliases = {len(scalars) + len(operands): 0}
        operands += (before,)
        in_specs += [pl.BlockSpec(memory_space=pl.ANY)]
    grid = pltpu.PrefetchScalarGridSpec(
        num_scalar_prefetch=len(scalars),
        grid=(1,),
        in_specs=in_specs,
        out_specs=pl.BlockSpec((peps, ROWW), lambda i, *_: (part, 0)),
        scratch_shapes=[pltpu.VMEM((STEP, 128), F32)]
        + [pltpu.VMEM(weight.shape, BF) for weight in large]
        + [pltpu.SemaphoreType.DMA((NL, len(large), PIECES))],
    )
    tokens_here = count * L // parts
    return pl.pallas_call(
        functools.partial(predict_kernel, part * peps),
        grid_spec=grid,
        out_shape=jax.ShapeDtypeStruct((count, ROWW), BF),
        input_output_aliases=aliases,
        compiler_params=pltpu.CompilerParams(vmem_limit_bytes=VMEM_LIMIT),
        cost_estimate=pl.CostEstimate(
            flops=2 * 12 * NL * tokens_here * D * D,
            bytes_accessed=4 * 2**20,
            transcendentals=2 * tokens_here * FF,
        ),
        name="predict",
    )(*scalars, *operands)


def slots_of(bins):
    count = bins.shape[1]
    across = jnp.broadcast_to(bins.astype(F32), (count, count))
    down = across.T
    earlier = (across == down) & (row_iota((count, count)) < lane_iota((count, count)))
    rank = jnp.sum(earlier.astype(F32), axis=0, keepdims=True)
    local = bins.astype(F32) - jnp.min(bins.astype(F32), axis=1, keepdims=True)
    return (local * QPB + rank).astype(jnp.int32)


def query_kernel(copies, bins_ref, spectra_ref, out_ref, ready_ref, sem):
    count = spectra_ref.shape[0]
    place = (row_iota((count, count)) == slots_of(bins_ref[...])).astype(BF)
    ready = standardize(spectra_ref[...].astype(F32))
    ready_ref[...] = jnp.dot(place, ready, preferred_element_type=F32).astype(BF)
    moves = [pltpu.make_async_copy(ready_ref, out_ref.at[i], sem.at[i]) for i in range(copies)]
    for move in moves:
        move.start()
    for move in moves:
        move.wait()


def prepare_queries(query_bin, spectra, copies):
    count = spectra.shape[0]
    return pl.pallas_call(
        functools.partial(query_kernel, copies),
        out_shape=jax.ShapeDtypeStruct((copies,) + spectra.shape, BF),
        out_specs=pl.BlockSpec(memory_space=pltpu.HBM),
        scratch_shapes=[pltpu.VMEM(spectra.shape, BF), pltpu.SemaphoreType.DMA((copies,))],
        compiler_params=pltpu.CompilerParams(vmem_limit_bytes=VMEM_LIMIT),
        name="prepare",
    )(query_bin.reshape(1, count), spectra)


def turn_kernel(mass_ref, *refs):
    sources, (side_ref, subs_ref) = refs[:-2], refs[-2:]
    count = sources[0].shape[0]
    per = 128 // count
    half = len(sources) * count
    me = mass_ref[0].astype(F32)
    for i in range(len(sources) // per):
        group = sources[i * per : (i + 1) * per]
        turned = jnp.concatenate([ref[:, :SPEC] for ref in group], axis=0).T
        lanes = pl.ds(i * 128, 128)
        side_ref[:, lanes] = turned
        for p in range(L):
            side_ref[p * ION : (p + 1) * ION, pl.ds(half + i * 128, 128)] = turned[
                (L - 1 - p) * ION : (L - p) * ION
            ]
        tags = jnp.concatenate([ref[:, SPEC:] for ref in group], axis=0).astype(F32).T
        for kind in range(2):
            owner, sub = tags[2 * kind : 2 * kind + 1], tags[2 * kind + 1 : 2 * kind + 2]
            sub = jnp.where(owner == me, sub, F32(-1.0))
            subs_ref[:, pl.ds(kind * half + i * 128, 128)] = jnp.broadcast_to(sub, (8, 128))


def turn(mass, sources):
    columns = 2 * len(sources) * sources[0].shape[0]
    return pl.pallas_call(
        turn_kernel,
        in_specs=[pl.BlockSpec(memory_space=pltpu.SMEM)]
        + [pl.BlockSpec(memory_space=pltpu.VMEM)] * len(sources),
        out_shape=(
            jax.ShapeDtypeStruct((SPEC, columns), BF),
            jax.ShapeDtypeStruct((8, columns), F32),
        ),
        compiler_params=pltpu.CompilerParams(vmem_limit_bytes=32 * 1024 * 1024),
        cost_estimate=pl.CostEstimate(flops=0, bytes_accessed=4 * 2**20, transcendentals=0),
        name="turn",
    )(mass, *sources)


def score_kernel(zs, seq_ref, side_ref, subs_ref, *refs):
    blocks, out_ref = refs[:-1], refs[-1]
    half = side_ref.shape[1] // 2
    y = lax.div(seq_ref[0], zs)
    low, row = lane_iota((8, 128)) < 32, row_iota((8, 128))
    for back, block in enumerate(blocks):
        queries = block[...]
        count = queries.shape[0]
        there = lax.rem(y + len(blocks) - back, len(blocks))
        bins = (row_iota((count, 128)) // QPB + there * (count // QPB)).astype(F32)
        best = []
        for kind in range(2):
            scores = jnp.dot(
                queries, side_ref[:, kind * half : (kind + 1) * half], preferred_element_type=F32
            )
            top = jnp.zeros((count, 128), F32)
            for i in range(half // 128):
                sub = subs_ref[:1, kind * half + i * 128 : kind * half + (i + 1) * 128]
                top = jnp.maximum(
                    top, jnp.where(sub == bins, scores[:, i * 128 : (i + 1) * 128], F32(0.0))
                )
            best.append(jnp.max(top.T, axis=0, keepdims=True) * F32(1.0 / math.sqrt(SPEC)))
        out = jnp.zeros((8, 128), F32)
        for z in range(zs):
            tile, shift = z // 4, 32 * (z % 4)
            pair = [jnp.broadcast_to(b[:, tile * 128 : (tile + 1) * 128], (8, 128)) for b in best]
            near = pltpu.roll(pair[0], (128 - shift) % 128, 1)
            far = pltpu.roll(pair[1], (128 - shift + 32) % 128, 1)
            out = jnp.where(row == z, jnp.where(low, near, far), out)
        out_ref[pl.ds(pl.multiple_of(there * zs, 8), zs), :] = out


def score(zs, seq, side, subs, blocks):
    inside = pl.BlockSpec(memory_space=pltpu.VMEM)
    queries = len(blocks) * blocks[0].shape[0]
    return pl.pallas_call(
        functools.partial(score_kernel, zs),
        in_specs=[pl.BlockSpec(memory_space=pltpu.SMEM)] + [inside] * (2 + len(blocks)),
        out_specs=inside,
        out_shape=jax.ShapeDtypeStruct((queries // 32, 128), F32),
        compiler_params=pltpu.CompilerParams(vmem_limit_bytes=32 * 1024 * 1024),
        name="score",
    )(seq, side, subs, *blocks)


def finish_kernel(bins_ref, pieces_ref, target_ref, decoy_ref):
    count = bins_ref.shape[1]
    best = jnp.maximum(jnp.max(pieces_ref[...], axis=0, keepdims=True), F32(0.0))
    slots = slots_of(bins_ref[...])
    place = row_iota((count, count)) == slots
    for kind, ref in enumerate((target_ref, decoy_ref)):
        wide = jnp.broadcast_to(best[:, kind * count : (kind + 1) * count], (count, count)).T
        ref[...] = jnp.sum(jnp.where(place, wide, F32(0.0)), axis=0, keepdims=True)


def finish(query_bin, pieces):
    count = query_bin.shape[0]
    shape = jax.ShapeDtypeStruct((1, count), F32)
    target, decoy = pl.pallas_call(finish_kernel, out_shape=(shape, shape), name="finish")(
        query_bin.reshape(1, count), pieces
    )
    return target.reshape(count), decoy.reshape(count)


def local(
    peptide_tokens,
    peptide_lengths,
    target_owner,
    target_sub,
    decoy_owner,
    decoy_sub,
    embedding,
    w_qkv,
    w_out,
    w_up,
    w_down,
    layer_gain,
    final_gain,
    w_head,
    query_spectra,
    query_bin,
):
    seqs = lax.axis_size("seq")
    ys, zs = YS, seqs // YS
    along_z = [[y * zs + z for z in range(zs)] for y in range(ys)]
    weights = (embedding, w_qkv, w_out, w_up, w_down, layer_gain, final_gain, w_head)
    owners = (target_owner, target_sub, decoy_owner, decoy_sub)
    queries = prepare_queries(query_bin, query_spectra, zs)
    queries = lax.all_to_all(
        queries, "seq", split_axis=0, concat_axis=0, tiled=True, axis_index_groups=along_z
    ).reshape(-1, SPEC)
    rows = predict_rows(0, 2, None, peptide_tokens, peptide_lengths, *owners, *weights)
    queries, rows, peptide_lengths = lax.optimization_barrier((queries, rows, peptide_lengths))
    ahead, back = [[(i, (i + d * zs) % seqs) for i in range(seqs)] for d in (1, ys - 1)]
    blocks = [queries, lax.ppermute(queries, "seq", ahead), None, lax.ppermute(queries, "seq", back)]
    rows = predict_rows(1, 2, rows, peptide_tokens, peptide_lengths, *owners, *weights)
    rows, blocks[1], blocks[3] = lax.optimization_barrier((rows, blocks[1], blocks[3]))
    blocks[2] = lax.ppermute(blocks[1], "seq", ahead)
    masses = lax.axis_size("mass")
    swap = [(i, i ^ 1) for i in range(masses)]
    held = [rows] + [
        lax.ppermute(rows, "mass", [(i, (i + d) % masses) for i in range(masses)])
        for d in range(2, masses, 2)
    ]
    held = held + [lax.ppermute(part, "mass", swap) for part in held]
    mass, seq = [lax.axis_index(axis).astype(jnp.int32).reshape(1) for axis in ("mass", "seq")]
    side, subs = turn(mass, held)
    pieces = score(zs, seq, side, subs, blocks)[:, None, :]
    pieces = lax.all_to_all(pieces, "seq", split_axis=0, concat_axis=0, tiled=True)[:, 0, :]
    return finish(query_bin, pieces)


def solution(mesh):
    in_specs = (
        P(("mass", "seq"), None),
        P(("mass", "seq")),
        P(("mass", "seq"), None),
        P(("mass", "seq")),
        P(("mass", "seq"), None),
        P(("mass", "seq")),
        P(),
        P(),
        P(),
        P(),
        P(),
        P(),
        P(),
        P(),
        P(("mass", "seq"), None),
        P(("mass", "seq")),
    )
    out_specs = (P(("mass", "seq")), P(("mass", "seq")))
    return jax.shard_map(local, mesh=mesh, in_specs=in_specs, out_specs=out_specs, check_vma=False)
```

```python
import functools
import math

import jax
import jax.numpy as jnp
import numpy as np
from jax import lax
from jax.experimental import pallas as pl
from jax.experimental.pallas import tpu as pltpu
from jax.sharding import PartitionSpec as P

HEADS = 8
L = 32
ION = 32
NL = 2
QPB = 4
YS = 4
D = 256
FF = 1024
SPEC = L * ION
EPS = 1e-06
BF = jnp.bfloat16
F32 = jnp.float32

STEP = 1024
TILE = 128
GROUP = 8
PIECES = 1
SHARES = 2
LAG = 0
ROWW = SPEC + 128
VMEM_LIMIT = 60 * 1024 * 1024
NT = (((1,), (1,)), ((), ()))


def sinusoid():
    place = np.arange(L, dtype=np.float32)[:, None]
    index = np.arange(D // 2, dtype=np.float32)[None, :]
    angle = place * np.exp(-math.log(10000.0) * 2.0 * index / D).astype(np.float32)
    return np.concatenate([np.sin(angle), np.cos(angle)], axis=1).astype(np.float32)


def lane_iota(shape):
    return lax.broadcasted_iota(jnp.int32, shape, len(shape) - 1)


def row_iota(shape):
    return lax.broadcasted_iota(jnp.int32, shape, len(shape) - 2)


def norm_rows(values, gain):
    scale = lax.rsqrt(jnp.mean(values * values, axis=-1, keepdims=True) + EPS)
    return (values * scale * gain).astype(BF)


def standardize(spectra):
    centred = spectra - jnp.mean(spectra, axis=-1, keepdims=True)
    return (centred * lax.rsqrt(jnp.mean(centred * centred, axis=-1, keepdims=True) + EPS)).astype(BF)


def gelu(x):
    inner = x * (math.sqrt(2 / math.pi) + (math.sqrt(2 / math.pi) * 0.044715) * (x * x))
    half = 0.5 * x
    return half + half * jnp.tanh(inner)


def feed_forward(state, normed, w_up_ref, w_down_ref):
    for c in range(0, FF, D):
        up = jnp.dot(normed, w_up_ref[:, c : c + D], preferred_element_type=F32)
        hidden = gelu(up).astype(BF)
        state = state + jnp.dot(hidden, w_down_ref[c : c + D, :], preferred_element_type=F32)
        yield
    return state


def attend(items):
    heads, peps = TILE // L, TILE // L
    lane = (lane_iota((L, heads * TILE)) % TILE) // L
    empty = jnp.zeros((L, TILE), BF)
    scores = []
    for query, key, _, _ in items:
        turned = query.T
        spread = [
            jnp.concatenate(
                [turned[h * L : (h + 1) * L] if h == i else empty for i in range(heads)], axis=1
            )
            for h in range(heads)
        ]
        spread = jnp.concatenate(spread, axis=0)
        scores.append(jnp.dot(key, spread, preferred_element_type=F32))
    yield
    wide = []
    for score, (_, _, _, length) in zip(scores, items):
        own = score[:L]
        for j in range(1, peps):
            own = jnp.where(lane == j, score[j * L : (j + 1) * L], own)
        own = own * (1.0 / math.sqrt(L))
        own = jnp.where(
            row_iota(own.shape) < jnp.concatenate([length] * heads, axis=1), own, F32(-1e30)
        )
        weights = jnp.exp(own - jnp.max(own, axis=0, keepdims=True))
        probs = weights * (1.0 / jnp.sum(weights, axis=0, keepdims=True))
        probs = probs.astype(BF)
        wide.append(
            jnp.concatenate(
                [jnp.where(lane == j, probs, jnp.zeros_like(probs)) for j in range(peps)], axis=0
            )
        )
    yield
    heard = []
    for probs, (_, _, value, _) in zip(wide, items):
        turned = value.T
        heard.append(
            jnp.concatenate(
                [
                    jnp.dot(
                        turned[h * L : (h + 1) * L],
                        probs[:, h * TILE : (h + 1) * TILE],
                        preferred_element_type=F32,
                    )
                    for h in range(heads)
                ],
                axis=0,
            )
        )
    yield
    return [out.T.astype(BF) for out in heard]


def transform(state, tile_lengths, refs, waits):
    w_qkv_ref, w_out_ref, w_up_ref, w_down_ref, gain_ref = refs
    for layer in range(NL):
        normed = norm_rows(state, gain_ref[layer, 0:1, :].astype(F32))
        waits(layer)
        mixed = [
            jnp.dot(
                normed, w_qkv_ref[layer, :, c * D : (c + 1) * D], preferred_element_type=F32
            ).astype(BF)
            for c in range(3)
        ]
        yield
        items = [
            [m[t * TILE : (t + 1) * TILE, g * TILE : (g + 1) * TILE] for m in mixed] + [tile_lengths[t]]
            for t in range(state.shape[0] // TILE)
            for g in range(D // TILE)
        ]
        heard = []
        for i in range(0, len(items), GROUP):
            heard = heard + (yield from attend(items[i : i + GROUP]))
        attended = jnp.concatenate(
            [jnp.concatenate(heard[i : i + 2], axis=1) for i in range(0, len(heard), 2)], axis=0
        )
        state = state + jnp.dot(attended, w_out_ref[layer], preferred_element_type=F32)
        normed = norm_rows(state, gain_ref[layer, 1:2, :].astype(F32))
        yield
        state = yield from feed_forward(state, normed, w_up_ref.at[layer], w_down_ref.at[layer])
    return state


def interleave(shares):
    results, step = [None] * len(shares), 0
    running = list(range(len(shares)))
    while running:
        for i in list(running):
            if step >= i * LAG:
                try:
                    next(shares[i])
                except StopIteration as stop:
                    results[i] = stop.value
                    running.remove(i)
        step += 1
    return results


def predict_kernel(
    base,
    lengths_ref,
    towner_ref,
    tsub_ref,
    downer_ref,
    dsub_ref,
    tokens_ref,
    embedding_ref,
    code_ref,
    w_qkv_ref,
    w_out_ref,
    w_up_ref,
    w_down_ref,
    gain_ref,
    final_ref,
    w_head_ref,
    *refs,
):
    rows_ref, logit_ref, sems = refs[-7], refs[-6], refs[-1]
    peps = STEP // L
    sources = (w_qkv_ref, w_out_ref, w_up_ref, w_down_ref)
    kept = refs[-5:-1]
    moves = [
        [
            pltpu.make_async_copy(
                source.at[layer, pl.ds(p * source.shape[1] // PIECES, source.shape[1] // PIECES)],
                held.at[layer, pl.ds(p * source.shape[1] // PIECES, source.shape[1] // PIECES)],
                sems.at[layer, i, p],
            )
            for i, (source, held) in enumerate(zip(sources, kept))
            for p in range(PIECES)
        ]
        for layer in range(NL)
    ]
    w_qkv_ref, w_out_ref, w_up_ref, w_down_ref = kept
    for move in moves[0] + moves[1]:
        move.start()

    first = base
    tokens = tokens_ref[...]
    tokens = jnp.concatenate([tokens] * (128 // tokens.shape[1]), axis=1)
    tokens = pltpu.roll(tokens, (128 - first) % 128, 1)
    vocab = embedding_ref.shape[0]
    onehot = jnp.concatenate(
        [tokens[:, j : j + 1] == lane_iota((L, vocab)) for j in range(peps)], axis=0
    ).astype(BF)
    state = jnp.dot(onehot, embedding_ref[...], preferred_element_type=F32)
    state = state + jnp.concatenate([code_ref[...]] * peps, axis=0)

    tile_lengths = []
    for t in range(STEP // TILE):
        lane = lane_iota((1, TILE)) // L
        vec = jnp.full((1, TILE), lengths_ref[first + t * 4], jnp.int32)
        for j in range(1, TILE // L):
            vec = jnp.where(lane == j, lengths_ref[first + t * 4 + j], vec)
        tile_lengths.append(vec)

    seen = set()

    def waits(layer):
        if layer not in seen:
            seen.add(layer)
            for move in moves[layer]:
                move.wait()

    share = STEP // SHARES
    refs = (w_qkv_ref, w_out_ref, w_up_ref, w_down_ref, gain_ref)
    state = interleave(
        [
            transform(
                state[i * share : (i + 1) * share],
                tile_lengths[i * share // TILE : (i + 1) * share // TILE],
                refs,
                waits,
            )
            for i in range(SHARES)
        ]
    )
    state = jnp.concatenate(state, axis=0)
    normed = norm_rows(state, final_ref[...].reshape(1, D).astype(F32))
    head = jnp.concatenate([w_head_ref[...]] * 4, axis=0)
    logit_ref[...] = lax.dot_general(normed, head, NT, preferred_element_type=F32)

    lane = lane_iota((peps, 128)) // ION
    tiles = []
    for t in range(SPEC // 128):
        tile = logit_ref[pl.ds(4 * t, peps, stride=L), :]
        for i in range(1, 4):
            tile = jnp.where(lane == i, logit_ref[pl.ds(4 * t + i, peps, stride=L), :], tile)
        tiles.append(tile)
    logits = jnp.concatenate(tiles, axis=1)
    intensity = 1.0 / (1.0 + jnp.exp(-logits))
    row = row_iota((peps, 128))
    column = lane_iota((peps, 128))
    length = jnp.zeros((peps, 128), jnp.int32)
    tag = jnp.zeros((peps, 128), jnp.int32)
    for i in range(peps):
        length = jnp.where(row == i, lengths_ref[first + i], length)
        for c, ref in enumerate((towner_ref, tsub_ref, downer_ref, dsub_ref)):
            tag = jnp.where((row == i) & (column == c), ref[first + i], tag)
    position = lane_iota((peps, SPEC)) // ION
    length = jnp.concatenate([length] * (SPEC // 128), axis=1)
    intensity = jnp.where(position < length - 1, intensity, F32(0.0))
    rows_ref[:, :SPEC] = standardize(intensity)
    rows_ref[:, SPEC:] = tag.astype(F32).astype(BF)


def predict_rows(
    part,
    parts,
    before,
    tokens,
    lengths,
    towner,
    tsub,
    downer,
    dsub,
    embedding,
    w_qkv,
    w_out,
    w_up,
    w_down,
    gains,
    final,
    w_head,
):
    count = tokens.shape[0]
    peps = STEP // L
    assert parts * peps == count
    whole = lambda shape: pl.BlockSpec(shape, lambda i, *_: (0,) * len(shape))
    operands = (
        tokens.T,
        embedding,
        jnp.asarray(sinusoid()),
        w_qkv,
        w_out,
        w_up,
        w_down,
        gains,
        final,
        w_head.T,
    )
    large = (w_qkv, w_out, w_up, w_down)
    in_specs = [
        pl.BlockSpec(memory_space=pltpu.HBM) if operand.ndim == 3 and operand is not gains else whole(operand.shape)
        for operand in operands
    ]
    scalars = (lengths, towner.reshape(count), tsub, downer.reshape(count), dsub)
    aliases = {}
    if before is not None:
        aliases = {len(scalars) + len(operands): 0}
        operands += (before,)
        in_specs += [pl.BlockSpec(memory_space=pl.ANY)]
    grid = pltpu.PrefetchScalarGridSpec(
        num_scalar_prefetch=0,
        grid=(1,),
        in_specs=[pl.BlockSpec(memory_space=pltpu.SMEM)] * len(scalars) + in_specs,
        out_specs=pl.BlockSpec((peps, ROWW), lambda i, *_: (part, 0)),
        scratch_shapes=[pltpu.VMEM((STEP, 128), F32)]
        + [pltpu.VMEM(weight.shape, BF) for weight in large]
        + [pltpu.SemaphoreType.DMA((NL, len(large), PIECES))],
    )
    tokens_here = count * L // parts
    return pl.pallas_call(
        functools.partial(predict_kernel, part * peps),
        grid_spec=grid,
        out_shape=jax.ShapeDtypeStruct((count, ROWW), BF),
        input_output_aliases=aliases,
        compiler_params=pltpu.CompilerParams(vmem_limit_bytes=VMEM_LIMIT),
        cost_estimate=pl.CostEstimate(
            flops=2 * 12 * NL * tokens_here * D * D,
            bytes_accessed=4 * 2**20,
            transcendentals=2 * tokens_here * FF,
        ),
        name="predict",
    )(*scalars, *operands)


def slots_of(bins):
    count = bins.shape[1]
    across = jnp.broadcast_to(bins.astype(F32), (count, count))
    down = across.T
    earlier = (across == down) & (row_iota((count, count)) < lane_iota((count, count)))
    rank = jnp.sum(earlier.astype(F32), axis=0, keepdims=True)
    local = bins.astype(F32) - jnp.min(bins.astype(F32), axis=1, keepdims=True)
    return (local * QPB + rank).astype(jnp.int32)


def query_kernel(copies, bins_ref, spectra_ref, out_ref, ready_ref, sem):
    count = spectra_ref.shape[0]
    place = (row_iota((count, count)) == slots_of(bins_ref[...])).astype(BF)
    ready = standardize(spectra_ref[...].astype(F32))
    ready_ref[...] = jnp.dot(place, ready, preferred_element_type=F32).astype(BF)
    moves = [pltpu.make_async_copy(ready_ref, out_ref.at[i], sem.at[i]) for i in range(copies)]
    for move in moves:
        move.start()
    for move in moves:
        move.wait()


def prepare_queries(query_bin, spectra, copies):
    count = spectra.shape[0]
    return pl.pallas_call(
        functools.partial(query_kernel, copies),
        out_shape=jax.ShapeDtypeStruct((copies,) + spectra.shape, BF),
        out_specs=pl.BlockSpec(memory_space=pltpu.HBM),
        scratch_shapes=[pltpu.VMEM(spectra.shape, BF), pltpu.SemaphoreType.DMA((copies,))],
        compiler_params=pltpu.CompilerParams(vmem_limit_bytes=VMEM_LIMIT),
        name="prepare",
    )(query_bin.reshape(1, count), spectra)


def turn_kernel(mass_ref, *refs):
    sources, (side_ref, subs_ref) = refs[:-2], refs[-2:]
    count = sources[0].shape[0]
    per = 128 // count
    half = len(sources) * count
    me = mass_ref[0].astype(F32)
    for i in range(len(sources) // per):
        group = sources[i * per : (i + 1) * per]
        turned = jnp.concatenate([ref[:, :SPEC] for ref in group], axis=0).T
        lanes = pl.ds(i * 128, 128)
        side_ref[:, lanes] = turned
        for p in range(L):
            side_ref[p * ION : (p + 1) * ION, pl.ds(half + i * 128, 128)] = turned[
                (L - 1 - p) * ION : (L - p) * ION
            ]
        tags = jnp.concatenate([ref[:, SPEC:] for ref in group], axis=0).astype(F32).T
        for kind in range(2):
            owner, sub = tags[2 * kind : 2 * kind + 1], tags[2 * kind + 1 : 2 * kind + 2]
            sub = jnp.where(owner == me, sub, F32(-1.0))
            subs_ref[:, pl.ds(kind * half + i * 128, 128)] = jnp.broadcast_to(sub, (8, 128))


def turn(mass, sources):
    columns = 2 * len(sources) * sources[0].shape[0]
    return pl.pallas_call(
        turn_kernel,
        in_specs=[pl.BlockSpec(memory_space=pltpu.SMEM)]
        + [pl.BlockSpec(memory_space=pltpu.VMEM)] * len(sources),
        out_shape=(
            jax.ShapeDtypeStruct((SPEC, columns), BF),
            jax.ShapeDtypeStruct((8, columns), F32),
        ),
        compiler_params=pltpu.CompilerParams(vmem_limit_bytes=32 * 1024 * 1024),
        cost_estimate=pl.CostEstimate(flops=0, bytes_accessed=4 * 2**20, transcendentals=0),
        name="turn",
    )(mass, *sources)


def score_kernel(zs, seq_ref, side_ref, subs_ref, *refs):
    blocks, out_ref = refs[:-1], refs[-1]
    half = side_ref.shape[1] // 2
    y = lax.div(seq_ref[0], zs)
    low, row = lane_iota((8, 128)) < 32, row_iota((8, 128))
    for back, block in enumerate(blocks):
        queries = block[...]
        count = queries.shape[0]
        there = lax.rem(y + len(blocks) - back, len(blocks))
        bins = (row_iota((count, 128)) // QPB + there * (count // QPB)).astype(F32)
        best = []
        for kind in range(2):
            scores = jnp.dot(
                queries, side_ref[:, kind * half : (kind + 1) * half], preferred_element_type=F32
            )
            top = jnp.zeros((count, 128), F32)
            for i in range(half // 128):
                sub = subs_ref[:1, kind * half + i * 128 : kind * half + (i + 1) * 128]
                top = jnp.maximum(
                    top, jnp.where(sub == bins, scores[:, i * 128 : (i + 1) * 128], F32(0.0))
                )
            best.append(jnp.max(top.T, axis=0, keepdims=True) * F32(1.0 / math.sqrt(SPEC)))
        out = jnp.zeros((8, 128), F32)
        for z in range(zs):
            tile, shift = z // 4, 32 * (z % 4)
            pair = [jnp.broadcast_to(b[:, tile * 128 : (tile + 1) * 128], (8, 128)) for b in best]
            near = pltpu.roll(pair[0], (128 - shift) % 128, 1)
            far = pltpu.roll(pair[1], (128 - shift + 32) % 128, 1)
            out = jnp.where(row == z, jnp.where(low, near, far), out)
        out_ref[pl.ds(pl.multiple_of(there * zs, 8), zs), :] = out


def score(zs, seq, side, subs, blocks):
    inside = pl.BlockSpec(memory_space=pltpu.VMEM)
    queries = len(blocks) * blocks[0].shape[0]
    return pl.pallas_call(
        functools.partial(score_kernel, zs),
        in_specs=[pl.BlockSpec(memory_space=pltpu.SMEM)] + [inside] * (2 + len(blocks)),
        out_specs=inside,
        out_shape=jax.ShapeDtypeStruct((queries // 32, 128), F32),
        compiler_params=pltpu.CompilerParams(vmem_limit_bytes=32 * 1024 * 1024),
        name="score",
    )(seq, side, subs, *blocks)


def finish_kernel(bins_ref, pieces_ref, target_ref, decoy_ref):
    count = bins_ref.shape[1]
    best = jnp.maximum(jnp.max(pieces_ref[...], axis=0, keepdims=True), F32(0.0))
    slots = slots_of(bins_ref[...])
    place = row_iota((count, count)) == slots
    for kind, ref in enumerate((target_ref, decoy_ref)):
        wide = jnp.broadcast_to(best[:, kind * count : (kind + 1) * count], (count, count)).T
        ref[...] = jnp.sum(jnp.where(place, wide, F32(0.0)), axis=0, keepdims=True)


def finish(query_bin, pieces):
    count = query_bin.shape[0]
    shape = jax.ShapeDtypeStruct((1, count), F32)
    target, decoy = pl.pallas_call(finish_kernel, out_shape=(shape, shape), name="finish")(
        query_bin.reshape(1, count), pieces
    )
    return target.reshape(count), decoy.reshape(count)


def local(
    peptide_tokens,
    peptide_lengths,
    target_owner,
    target_sub,
    decoy_owner,
    decoy_sub,
    embedding,
    w_qkv,
    w_out,
    w_up,
    w_down,
    layer_gain,
    final_gain,
    w_head,
    query_spectra,
    query_bin,
):
    seqs = lax.axis_size("seq")
    ys, zs = YS, seqs // YS
    along_z = [[y * zs + z for z in range(zs)] for y in range(ys)]
    weights = (embedding, w_qkv, w_out, w_up, w_down, layer_gain, final_gain, w_head)
    owners = (target_owner, target_sub, decoy_owner, decoy_sub)
    queries = prepare_queries(query_bin, query_spectra, zs)
    queries = lax.all_to_all(
        queries, "seq", split_axis=0, concat_axis=0, tiled=True, axis_index_groups=along_z
    ).reshape(-1, SPEC)
    rows = predict_rows(0, 2, None, peptide_tokens, peptide_lengths, *owners, *weights)
    queries, rows, peptide_lengths = lax.optimization_barrier((queries, rows, peptide_lengths))
    ahead, back = [[(i, (i + d * zs) % seqs) for i in range(seqs)] for d in (1, ys - 1)]
    blocks = [queries, lax.ppermute(queries, "seq", ahead), None, lax.ppermute(queries, "seq", back)]
    rows = predict_rows(1, 2, rows, peptide_tokens, peptide_lengths, *owners, *weights)
    rows, blocks[1], blocks[3] = lax.optimization_barrier((rows, blocks[1], blocks[3]))
    blocks[2] = lax.ppermute(blocks[1], "seq", ahead)
    masses = lax.axis_size("mass")
    swap = [(i, i ^ 1) for i in range(masses)]
    held = [rows] + [
        lax.ppermute(rows, "mass", [(i, (i + d) % masses) for i in range(masses)])
        for d in range(2, masses, 2)
    ]
    held = held + [lax.ppermute(part, "mass", swap) for part in held]
    mass, seq = [lax.axis_index(axis).astype(jnp.int32).reshape(1) for axis in ("mass", "seq")]
    side, subs = turn(mass, held)
    pieces = score(zs, seq, side, subs, blocks)[:, None, :]
    pieces = lax.all_to_all(pieces, "seq", split_axis=0, concat_axis=0, tiled=True)[:, 0, :]
    return finish(query_bin, pieces)


def solution(mesh):
    in_specs = (
        P(("mass", "seq"), None),
        P(("mass", "seq")),
        P(("mass", "seq"), None),
        P(("mass", "seq")),
        P(("mass", "seq"), None),
        P(("mass", "seq")),
        P(),
        P(),
        P(),
        P(),
        P(),
        P(),
        P(),
        P(),
        P(("mass", "seq"), None),
        P(("mass", "seq")),
    )
    out_specs = (P(("mass", "seq")), P(("mass", "seq")))
    return jax.shard_map(local, mesh=mesh, in_specs=in_specs, out_specs=out_specs, check_vma=False)
```

```python
import functools
import math

import jax
import jax.numpy as jnp
import numpy as np
from jax import lax
from jax.experimental import pallas as pl
from jax.experimental.pallas import tpu as pltpu
from jax.sharding import PartitionSpec as P

HEADS = 8
L = 32
ION = 32
NL = 2
QPB = 4
YS = 4
D = 256
FF = 1024
SPEC = L * ION
EPS = 1e-06
BF = jnp.bfloat16
F32 = jnp.float32

STEP = 1024
TILE = 128
GROUP = 8
PIECES = 1
SHARES = 2
LAG = 0
LAST = SPEC - ION
VMEM_LIMIT = 60 * 1024 * 1024
NT = (((1,), (1,)), ((), ()))


def sinusoid():
    place = np.arange(L, dtype=np.float32)[:, None]
    index = np.arange(D // 2, dtype=np.float32)[None, :]
    angle = place * np.exp(-math.log(10000.0) * 2.0 * index / D).astype(np.float32)
    return np.concatenate([np.sin(angle), np.cos(angle)], axis=1).astype(np.float32)


def lane_iota(shape):
    return lax.broadcasted_iota(jnp.int32, shape, len(shape) - 1)


def row_iota(shape):
    return lax.broadcasted_iota(jnp.int32, shape, len(shape) - 2)


def norm_rows(values, gain):
    scale = lax.rsqrt(jnp.mean(values * values, axis=-1, keepdims=True) + EPS)
    return (values * scale * gain).astype(BF)


def standardize(spectra):
    centred = spectra - jnp.mean(spectra, axis=-1, keepdims=True)
    return (centred * lax.rsqrt(jnp.mean(centred * centred, axis=-1, keepdims=True) + EPS)).astype(BF)


def gelu(x):
    inner = x * (math.sqrt(2 / math.pi) + (math.sqrt(2 / math.pi) * 0.044715) * (x * x))
    half = 0.5 * x
    return half + half * jnp.tanh(inner)


def feed_forward(state, normed, w_up_ref, w_down_ref):
    for c in range(0, FF, D):
        up = jnp.dot(normed, w_up_ref[:, c : c + D], preferred_element_type=F32)
        hidden = gelu(up).astype(BF)
        state = state + jnp.dot(hidden, w_down_ref[c : c + D, :], preferred_element_type=F32)
        yield
    return state


def attend(items):
    heads, peps = TILE // L, TILE // L
    lane = (lane_iota((L, heads * TILE)) % TILE) // L
    empty = jnp.zeros((L, TILE), BF)
    scores = []
    for query, key, _, _ in items:
        turned = query.T
        spread = [
            jnp.concatenate(
                [turned[h * L : (h + 1) * L] if h == i else empty for i in range(heads)], axis=1
            )
            for h in range(heads)
        ]
        spread = jnp.concatenate(spread, axis=0)
        scores.append(jnp.dot(key, spread, preferred_element_type=F32))
    yield
    wide = []
    for score, (_, _, _, length) in zip(scores, items):
        own = score[:L]
        for j in range(1, peps):
            own = jnp.where(lane == j, score[j * L : (j + 1) * L], own)
        own = own * (1.0 / math.sqrt(L))
        own = jnp.where(
            row_iota(own.shape) < jnp.concatenate([length] * heads, axis=1), own, F32(-1e30)
        )
        weights = jnp.exp(own - jnp.max(own, axis=0, keepdims=True))
        probs = weights * (1.0 / jnp.sum(weights, axis=0, keepdims=True))
        probs = probs.astype(BF)
        wide.append(
            jnp.concatenate(
                [jnp.where(lane == j, probs, jnp.zeros_like(probs)) for j in range(peps)], axis=0
            )
        )
    yield
    heard = []
    for probs, (_, _, value, _) in zip(wide, items):
        turned = value.T
        heard.append(
            jnp.concatenate(
                [
                    jnp.dot(
                        turned[h * L : (h + 1) * L],
                        probs[:, h * TILE : (h + 1) * TILE],
                        preferred_element_type=F32,
                    )
                    for h in range(heads)
                ],
                axis=0,
            )
        )
    yield
    return [out.T.astype(BF) for out in heard]


def transform(state, tile_lengths, refs, waits):
    w_qkv_ref, w_out_ref, w_up_ref, w_down_ref, gain_ref = refs
    for layer in range(NL):
        normed = norm_rows(state, gain_ref[layer, 0:1, :].astype(F32))
        waits(layer)
        mixed = [
            jnp.dot(
                normed, w_qkv_ref[layer, :, c * D : (c + 1) * D], preferred_element_type=F32
            ).astype(BF)
            for c in range(3)
        ]
        yield
        items = [
            [m[t * TILE : (t + 1) * TILE, g * TILE : (g + 1) * TILE] for m in mixed] + [tile_lengths[t]]
            for t in range(state.shape[0] // TILE)
            for g in range(D // TILE)
        ]
        heard = []
        for i in range(0, len(items), GROUP):
            heard = heard + (yield from attend(items[i : i + GROUP]))
        attended = jnp.concatenate(
            [jnp.concatenate(heard[i : i + 2], axis=1) for i in range(0, len(heard), 2)], axis=0
        )
        state = state + jnp.dot(attended, w_out_ref[layer], preferred_element_type=F32)
        normed = norm_rows(state, gain_ref[layer, 1:2, :].astype(F32))
        yield
        state = yield from feed_forward(state, normed, w_up_ref.at[layer], w_down_ref.at[layer])
    return state


def interleave(shares):
    results, step = [None] * len(shares), 0
    running = list(range(len(shares)))
    while running:
        for i in list(running):
            if step >= i * LAG:
                try:
                    next(shares[i])
                except StopIteration as stop:
                    results[i] = stop.value
                    running.remove(i)
        step += 1
    return results


def predict_kernel(
    base,
    lengths_ref,
    towner_ref,
    tsub_ref,
    downer_ref,
    dsub_ref,
    tokens_ref,
    embedding_ref,
    code_ref,
    w_qkv_ref,
    w_out_ref,
    w_up_ref,
    w_down_ref,
    gain_ref,
    final_ref,
    w_head_ref,
    *refs,
):
    rows_ref, logit_ref, sems = refs[-7], refs[-6], refs[-1]
    peps = STEP // L
    sources = (w_qkv_ref, w_out_ref, w_up_ref, w_down_ref)
    kept = refs[-5:-1]
    moves = [
        [
            pltpu.make_async_copy(
                source.at[layer, pl.ds(p * source.shape[1] // PIECES, source.shape[1] // PIECES)],
                held.at[layer, pl.ds(p * source.shape[1] // PIECES, source.shape[1] // PIECES)],
                sems.at[layer, i, p],
            )
            for i, (source, held) in enumerate(zip(sources, kept))
            for p in range(PIECES)
        ]
        for layer in range(NL)
    ]
    w_qkv_ref, w_out_ref, w_up_ref, w_down_ref = kept
    for move in moves[0] + moves[1]:
        move.start()

    first = base
    tokens = tokens_ref[...]
    tokens = jnp.concatenate([tokens] * (128 // tokens.shape[1]), axis=1)
    tokens = pltpu.roll(tokens, (128 - first) % 128, 1)
    vocab = embedding_ref.shape[0]
    onehot = jnp.concatenate(
        [tokens[:, j : j + 1] == lane_iota((L, vocab)) for j in range(peps)], axis=0
    ).astype(BF)
    state = jnp.dot(onehot, embedding_ref[...], preferred_element_type=F32)
    state = state + jnp.concatenate([code_ref[...]] * peps, axis=0)

    tile_lengths = []
    for t in range(STEP // TILE):
        lane = lane_iota((1, TILE)) // L
        vec = jnp.full((1, TILE), lengths_ref[first + t * 4], jnp.int32)
        for j in range(1, TILE // L):
            vec = jnp.where(lane == j, lengths_ref[first + t * 4 + j], vec)
        tile_lengths.append(vec)

    seen = set()

    def waits(layer):
        if layer not in seen:
            seen.add(layer)
            for move in moves[layer]:
                move.wait()

    share = STEP // SHARES
    refs = (w_qkv_ref, w_out_ref, w_up_ref, w_down_ref, gain_ref)
    state = interleave(
        [
            transform(
                state[i * share : (i + 1) * share],
                tile_lengths[i * share // TILE : (i + 1) * share // TILE],
                refs,
                waits,
            )
            for i in range(SHARES)
        ]
    )
    state = jnp.concatenate(state, axis=0)
    normed = norm_rows(state, final_ref[...].reshape(1, D).astype(F32))
    head = jnp.concatenate([w_head_ref[...]] * 4, axis=0)
    logit_ref[...] = lax.dot_general(normed, head, NT, preferred_element_type=F32)

    lane = lane_iota((peps, 128)) // ION
    tiles = []
    for t in range(SPEC // 128):
        tile = logit_ref[pl.ds(4 * t, peps, stride=L), :]
        for i in range(1, 4):
            tile = jnp.where(lane == i, logit_ref[pl.ds(4 * t + i, peps, stride=L), :], tile)
        tiles.append(tile)
    logits = jnp.concatenate(tiles, axis=1)
    intensity = 1.0 / (1.0 + jnp.exp(-logits))
    row = row_iota((peps, 128))
    column = lane_iota((peps, 128))
    length = jnp.zeros((peps, 128), jnp.int32)
    tag = jnp.zeros((peps, 128), jnp.int32)
    for i in range(peps):
        length = jnp.where(row == i, lengths_ref[first + i], length)
        for c, ref in enumerate((towner_ref, tsub_ref, downer_ref, dsub_ref)):
            tag = jnp.where((row == i) & (column == LAST % 128 + 1 + c), ref[first + i], tag)
    position = lane_iota((peps, SPEC)) // ION
    length = jnp.concatenate([length] * (SPEC // 128), axis=1)
    intensity = jnp.where(position < length - 1, intensity, F32(0.0))
    spectra = standardize(intensity)
    rows_ref[:, : SPEC - 128] = spectra[:, : SPEC - 128]
    rows_ref[:, SPEC - 128 :] = jnp.where(
        (column > LAST % 128) & (column <= LAST % 128 + 4),
        tag.astype(F32).astype(BF),
        spectra[:, SPEC - 128 :],
    )


def predict_rows(
    part,
    parts,
    before,
    tokens,
    lengths,
    towner,
    tsub,
    downer,
    dsub,
    embedding,
    w_qkv,
    w_out,
    w_up,
    w_down,
    gains,
    final,
    w_head,
):
    count = tokens.shape[0]
    peps = STEP // L
    assert parts * peps == count
    whole = lambda shape: pl.BlockSpec(shape, lambda i, *_: (0,) * len(shape))
    operands = (
        tokens.T,
        embedding,
        jnp.asarray(sinusoid()),
        w_qkv,
        w_out,
        w_up,
        w_down,
        gains,
        final,
        w_head.T,
    )
    large = (w_qkv, w_out, w_up, w_down)
    in_specs = [
        pl.BlockSpec(memory_space=pltpu.HBM) if operand.ndim == 3 and operand is not gains else whole(operand.shape)
        for operand in operands
    ]
    scalars = (lengths, towner.reshape(count), tsub, downer.reshape(count), dsub)
    aliases = {}
    if before is not None:
        aliases = {len(scalars) + len(operands): 0}
        operands += (before,)
        in_specs += [pl.BlockSpec(memory_space=pl.ANY)]
    grid = pltpu.PrefetchScalarGridSpec(
        num_scalar_prefetch=0,
        grid=(1,),
        in_specs=[pl.BlockSpec(memory_space=pltpu.SMEM)] * len(scalars) + in_specs,
        out_specs=pl.BlockSpec((peps, SPEC), lambda i, *_: (part, 0)),
        scratch_shapes=[pltpu.VMEM((STEP, 128), F32)]
        + [pltpu.VMEM(weight.shape, BF) for weight in large]
        + [pltpu.SemaphoreType.DMA((NL, len(large), PIECES))],
    )
    tokens_here = count * L // parts
    return pl.pallas_call(
        functools.partial(predict_kernel, part * peps),
        grid_spec=grid,
        out_shape=jax.ShapeDtypeStruct((count, SPEC), BF),
        input_output_aliases=aliases,
        compiler_params=pltpu.CompilerParams(vmem_limit_bytes=VMEM_LIMIT),
        cost_estimate=pl.CostEstimate(
            flops=2 * 12 * NL * tokens_here * D * D,
            bytes_accessed=4 * 2**20,
            transcendentals=2 * tokens_here * FF,
        ),
        name="predict",
    )(*scalars, *operands)


def slots_of(bins):
    count = bins.shape[1]
    across = jnp.broadcast_to(bins.astype(F32), (count, count))
    down = across.T
    earlier = (across == down) & (row_iota((count, count)) < lane_iota((count, count)))
    rank = jnp.sum(earlier.astype(F32), axis=0, keepdims=True)
    local = bins.astype(F32) - jnp.min(bins.astype(F32), axis=1, keepdims=True)
    return (local * QPB + rank).astype(jnp.int32)


def query_kernel(copies, bins_ref, spectra_ref, out_ref, ready_ref, sem):
    count = spectra_ref.shape[0]
    place = (row_iota((count, count)) == slots_of(bins_ref[...])).astype(BF)
    ready = standardize(spectra_ref[...].astype(F32))
    ready_ref[...] = jnp.dot(place, ready, preferred_element_type=F32).astype(BF)
    moves = [pltpu.make_async_copy(ready_ref, out_ref.at[i], sem.at[i]) for i in range(copies)]
    for move in moves:
        move.start()
    for move in moves:
        move.wait()


def prepare_queries(query_bin, spectra, copies):
    count = spectra.shape[0]
    return pl.pallas_call(
        functools.partial(query_kernel, copies),
        out_shape=jax.ShapeDtypeStruct((copies,) + spectra.shape, BF),
        out_specs=pl.BlockSpec(memory_space=pltpu.HBM),
        scratch_shapes=[pltpu.VMEM(spectra.shape, BF), pltpu.SemaphoreType.DMA((copies,))],
        compiler_params=pltpu.CompilerParams(vmem_limit_bytes=VMEM_LIMIT),
        name="prepare",
    )(query_bin.reshape(1, count), spectra)


def turn_kernel(mass_ref, *refs):
    sources, (side_ref, subs_ref) = refs[:-2], refs[-2:]
    per = 128 // sources[0].shape[0]
    half = side_ref.shape[1] // 2
    me = mass_ref[0].astype(F32)
    for i in range(len(sources) // per):
        turned = jnp.concatenate([ref[...] for ref in sources[i * per : (i + 1) * per]], axis=0).T
        last = turned[LAST : LAST + 16].astype(F32)
        background = jnp.broadcast_to(last[:1], (ION, 128)).astype(BF)
        targets, decoys = pl.ds(i * 128, 128), pl.ds(half + i * 128, 128)
        side_ref[:LAST, targets] = turned[:LAST]
        side_ref[LAST:, targets] = background
        side_ref[:ION, decoys] = background
        for p in range(1, L):
            side_ref[p * ION : (p + 1) * ION, decoys] = turned[(L - 1 - p) * ION : (L - p) * ION]
        for kind, lanes in enumerate((targets, decoys)):
            owner, sub = last[1 + 2 * kind : 2 + 2 * kind], last[2 + 2 * kind : 3 + 2 * kind]
            sub = jnp.where(owner == me, sub, F32(-1.0))
            subs_ref[:, lanes] = jnp.broadcast_to(sub, (8, 128))


def turn(mass, sources):
    columns = 2 * len(sources) * sources[0].shape[0]
    return pl.pallas_call(
        turn_kernel,
        in_specs=[pl.BlockSpec(memory_space=pltpu.SMEM)]
        + [pl.BlockSpec(memory_space=pltpu.VMEM)] * len(sources),
        out_shape=(
            jax.ShapeDtypeStruct((SPEC, columns), BF),
            jax.ShapeDtypeStruct((8, columns), F32),
        ),
        compiler_params=pltpu.CompilerParams(vmem_limit_bytes=32 * 1024 * 1024),
        cost_estimate=pl.CostEstimate(flops=0, bytes_accessed=4 * 2**20, transcendentals=0),
        name="turn",
    )(mass, *sources)


def score_kernel(zs, sides, seq_ref, *refs):
    turned, blocks, out_ref = refs[: 2 * sides], refs[2 * sides : -1], refs[-1]
    y = lax.div(seq_ref[0], zs)
    low, row = lane_iota((8, 128)) < 32, row_iota((8, 128))
    for back, block in enumerate(blocks):
        queries = block[...]
        count = queries.shape[0]
        there = lax.rem(y + len(blocks) - back, len(blocks))
        bins = (row_iota((count, 128)) // QPB + there * (count // QPB)).astype(F32)
        tops = [jnp.zeros((count, 128), F32) for _ in range(2)]
        for side_ref, subs_ref in zip(turned[0::2], turned[1::2]):
            scores = jnp.dot(queries, side_ref[...], preferred_element_type=F32)
            tiles = scores.shape[1] // 128
            for i in range(tiles):
                kind = 2 * i // tiles
                own = jnp.where(
                    subs_ref[:1, i * 128 : (i + 1) * 128] == bins,
                    scores[:, i * 128 : (i + 1) * 128],
                    F32(0.0),
                )
                tops[kind] = jnp.maximum(tops[kind], own)
        best = [jnp.max(top.T, axis=0, keepdims=True) * F32(1.0 / math.sqrt(SPEC)) for top in tops]
        out = jnp.zeros((8, 128), F32)
        for z in range(zs):
            tile, shift = z // 4, 32 * (z % 4)
            pair = [jnp.broadcast_to(b[:, tile * 128 : (tile + 1) * 128], (8, 128)) for b in best]
            near = pltpu.roll(pair[0], (128 - shift) % 128, 1)
            far = pltpu.roll(pair[1], (128 - shift + 32) % 128, 1)
            out = jnp.where(row == z, jnp.where(low, near, far), out)
        out_ref[pl.ds(pl.multiple_of(there * zs, 8), zs), :] = out


def score(zs, seq, sides, blocks):
    inside = pl.BlockSpec(memory_space=pltpu.VMEM)
    queries = len(blocks) * blocks[0].shape[0]
    return pl.pallas_call(
        functools.partial(score_kernel, zs, len(sides)),
        in_specs=[pl.BlockSpec(memory_space=pltpu.SMEM)] + [inside] * (2 * len(sides) + len(blocks)),
        out_specs=inside,
        out_shape=jax.ShapeDtypeStruct((queries // 32, 128), F32),
        compiler_params=pltpu.CompilerParams(vmem_limit_bytes=32 * 1024 * 1024),
        name="score",
    )(seq, *[part for side in sides for part in side], *blocks)


def finish_kernel(bins_ref, pieces_ref, target_ref, decoy_ref):
    count = bins_ref.shape[1]
    best = jnp.maximum(jnp.max(pieces_ref[...], axis=0, keepdims=True), F32(0.0))
    slots = slots_of(bins_ref[...])
    place = row_iota((count, count)) == slots
    for kind, ref in enumerate((target_ref, decoy_ref)):
        wide = jnp.broadcast_to(best[:, kind * count : (kind + 1) * count], (count, count)).T
        ref[...] = jnp.sum(jnp.where(place, wide, F32(0.0)), axis=0, keepdims=True)


def finish(query_bin, pieces):
    count = query_bin.shape[0]
    shape = jax.ShapeDtypeStruct((1, count), F32)
    target, decoy = pl.pallas_call(finish_kernel, out_shape=(shape, shape), name="finish")(
        query_bin.reshape(1, count), pieces
    )
    return target.reshape(count), decoy.reshape(count)


def local(
    peptide_tokens,
    peptide_lengths,
    target_owner,
    target_sub,
    decoy_owner,
    decoy_sub,
    embedding,
    w_qkv,
    w_out,
    w_up,
    w_down,
    layer_gain,
    final_gain,
    w_head,
    query_spectra,
    query_bin,
):
    seqs = lax.axis_size("seq")
    ys, zs = YS, seqs // YS
    along_z = [[y * zs + z for z in range(zs)] for y in range(ys)]
    weights = (embedding, w_qkv, w_out, w_up, w_down, layer_gain, final_gain, w_head)
    owners = (target_owner, target_sub, decoy_owner, decoy_sub)
    queries = prepare_queries(query_bin, query_spectra, zs)
    queries = lax.all_to_all(
        queries, "seq", split_axis=0, concat_axis=0, tiled=True, axis_index_groups=along_z
    ).reshape(-1, SPEC)
    rows = predict_rows(0, 2, None, peptide_tokens, peptide_lengths, *owners, *weights)
    queries, rows, peptide_lengths = lax.optimization_barrier((queries, rows, peptide_lengths))
    ahead, back = [[(i, (i + d * zs) % seqs) for i in range(seqs)] for d in (1, ys - 1)]
    blocks = [queries, lax.ppermute(queries, "seq", ahead), None, lax.ppermute(queries, "seq", back)]
    rows = predict_rows(1, 2, rows, peptide_tokens, peptide_lengths, *owners, *weights)
    rows, blocks[1], blocks[3] = lax.optimization_barrier((rows, blocks[1], blocks[3]))
    blocks[2] = lax.ppermute(blocks[1], "seq", ahead)
    masses = lax.axis_size("mass")
    swap = [(i, i ^ 1) for i in range(masses)]
    far = [
        lax.ppermute(rows, "mass", [(i, (i + d) % masses) for i in range(masses)])
        for d in range(2, masses, 2)
    ]
    near = [rows, lax.ppermute(rows, "mass", swap)]
    far = far + [lax.ppermute(part, "mass", swap) for part in far]
    mass, seq = [lax.axis_index(axis).astype(jnp.int32).reshape(1) for axis in ("mass", "seq")]
    pieces = score(zs, seq, [turn(mass, near), turn(mass, far)], blocks)[:, None, :]
    pieces = lax.all_to_all(pieces, "seq", split_axis=0, concat_axis=0, tiled=True)[:, 0, :]
    return finish(query_bin, pieces)


def solution(mesh):
    in_specs = (
        P(("mass", "seq"), None),
        P(("mass", "seq")),
        P(("mass", "seq"), None),
        P(("mass", "seq")),
        P(("mass", "seq"), None),
        P(("mass", "seq")),
        P(),
        P(),
        P(),
        P(),
        P(),
        P(),
        P(),
        P(),
        P(("mass", "seq"), None),
        P(("mass", "seq")),
    )
    out_specs = (P(("mass", "seq")), P(("mass", "seq")))
    return jax.shard_map(local, mesh=mesh, in_specs=in_specs, out_specs=out_specs, check_vma=False)
```

```python
import functools
import math

import jax
import jax.numpy as jnp
import numpy as np
from jax import lax
from jax.experimental import pallas as pl
from jax.experimental.pallas import tpu as pltpu
from jax.sharding import PartitionSpec as P

HEADS = 8
L = 32
ION = 32
NL = 2
QPB = 4
YS = 4
D = 256
FF = 1024
SPEC = L * ION
EPS = 1e-06
BF = jnp.bfloat16
F32 = jnp.float32

STEP = 1024
TILE = 128
GROUP = 8
PIECES = 1
SHARES = 2
LAG = 0
LAST = SPEC - ION
VMEM_LIMIT = 60 * 1024 * 1024
NT = (((1,), (1,)), ((), ()))


def sinusoid():
    place = np.arange(L, dtype=np.float32)[:, None]
    index = np.arange(D // 2, dtype=np.float32)[None, :]
    angle = place * np.exp(-math.log(10000.0) * 2.0 * index / D).astype(np.float32)
    return np.concatenate([np.sin(angle), np.cos(angle)], axis=1).astype(np.float32)


def lane_iota(shape):
    return lax.broadcasted_iota(jnp.int32, shape, len(shape) - 1)


def row_iota(shape):
    return lax.broadcasted_iota(jnp.int32, shape, len(shape) - 2)


def norm_rows(values, gain):
    scale = lax.rsqrt(jnp.mean(values * values, axis=-1, keepdims=True) + EPS)
    return (values * scale * gain).astype(BF)


def standardize(spectra):
    centred = spectra - jnp.mean(spectra, axis=-1, keepdims=True)
    return (centred * lax.rsqrt(jnp.mean(centred * centred, axis=-1, keepdims=True) + EPS)).astype(BF)


def gelu(x):
    inner = x * (math.sqrt(2 / math.pi) + (math.sqrt(2 / math.pi) * 0.044715) * (x * x))
    half = 0.5 * x
    return half + half * jnp.tanh(inner)


def feed_forward(state, normed, w_up_ref, w_down_ref):
    for c in range(0, FF, D):
        up = jnp.dot(normed, w_up_ref[:, c : c + D], preferred_element_type=F32)
        hidden = gelu(up).astype(BF)
        state = state + jnp.dot(hidden, w_down_ref[c : c + D, :], preferred_element_type=F32)
        yield
    return state


def attend(items):
    heads, peps = TILE // L, TILE // L
    lane = (lane_iota((L, heads * TILE)) % TILE) // L
    empty = jnp.zeros((L, TILE), BF)
    scores = []
    for query, key, _, _ in items:
        turned = query.T
        spread = [
            jnp.concatenate(
                [turned[h * L : (h + 1) * L] if h == i else empty for i in range(heads)], axis=1
            )
            for h in range(heads)
        ]
        spread = jnp.concatenate(spread, axis=0)
        scores.append(jnp.dot(key, spread, preferred_element_type=F32))
    yield
    wide = []
    for score, (_, _, _, length) in zip(scores, items):
        own = score[:L]
        for j in range(1, peps):
            own = jnp.where(lane == j, score[j * L : (j + 1) * L], own)
        own = own * (1.0 / math.sqrt(L))
        own = jnp.where(
            row_iota(own.shape) < jnp.concatenate([length] * heads, axis=1), own, F32(-1e30)
        )
        weights = jnp.exp(own - jnp.max(own, axis=0, keepdims=True))
        probs = weights * (1.0 / jnp.sum(weights, axis=0, keepdims=True))
        probs = probs.astype(BF)
        wide.append(
            jnp.concatenate(
                [jnp.where(lane == j, probs, jnp.zeros_like(probs)) for j in range(peps)], axis=0
            )
        )
    yield
    heard = []
    for probs, (_, _, value, _) in zip(wide, items):
        turned = value.T
        heard.append(
            jnp.concatenate(
                [
                    jnp.dot(
                        turned[h * L : (h + 1) * L],
                        probs[:, h * TILE : (h + 1) * TILE],
                        preferred_element_type=F32,
                    )
                    for h in range(heads)
                ],
                axis=0,
            )
        )
    yield
    return [out.T.astype(BF) for out in heard]


def transform(state, tile_lengths, refs, waits):
    w_qkv_ref, w_out_ref, w_up_ref, w_down_ref, gain_ref = refs
    for layer in range(NL):
        normed = norm_rows(state, gain_ref[layer, 0:1, :].astype(F32))
        waits(layer)
        mixed = [
            jnp.dot(
                normed, w_qkv_ref[layer, :, c * D : (c + 1) * D], preferred_element_type=F32
            ).astype(BF)
            for c in range(3)
        ]
        yield
        items = [
            [m[t * TILE : (t + 1) * TILE, g * TILE : (g + 1) * TILE] for m in mixed] + [tile_lengths[t]]
            for t in range(state.shape[0] // TILE)
            for g in range(D // TILE)
        ]
        heard = []
        for i in range(0, len(items), GROUP):
            heard = heard + (yield from attend(items[i : i + GROUP]))
        attended = jnp.concatenate(
            [jnp.concatenate(heard[i : i + 2], axis=1) for i in range(0, len(heard), 2)], axis=0
        )
        state = state + jnp.dot(attended, w_out_ref[layer], preferred_element_type=F32)
        normed = norm_rows(state, gain_ref[layer, 1:2, :].astype(F32))
        yield
        state = yield from feed_forward(state, normed, w_up_ref.at[layer], w_down_ref.at[layer])
    return state


def interleave(shares):
    results, step = [None] * len(shares), 0
    running = list(range(len(shares)))
    while running:
        for i in list(running):
            if step >= i * LAG:
                try:
                    next(shares[i])
                except StopIteration as stop:
                    results[i] = stop.value
                    running.remove(i)
        step += 1
    return results


def predict_kernel(
    base,
    lengths_ref,
    towner_ref,
    tsub_ref,
    downer_ref,
    dsub_ref,
    tokens_ref,
    embedding_ref,
    code_ref,
    w_qkv_ref,
    w_out_ref,
    w_up_ref,
    w_down_ref,
    gain_ref,
    final_ref,
    w_head_ref,
    *refs,
):
    rows_ref, logit_ref, sems = refs[-7], refs[-6], refs[-1]
    peps = STEP // L
    sources = (w_qkv_ref, w_out_ref, w_up_ref, w_down_ref)
    kept = refs[-5:-1]
    moves = [
        [
            pltpu.make_async_copy(
                source.at[layer, pl.ds(p * source.shape[1] // PIECES, source.shape[1] // PIECES)],
                held.at[layer, pl.ds(p * source.shape[1] // PIECES, source.shape[1] // PIECES)],
                sems.at[layer, i, p],
            )
            for i, (source, held) in enumerate(zip(sources, kept))
            for p in range(PIECES)
        ]
        for layer in range(NL)
    ]
    w_qkv_ref, w_out_ref, w_up_ref, w_down_ref = kept
    for move in moves[0] + moves[1]:
        move.start()

    first = base
    tokens = tokens_ref[...]
    tokens = jnp.concatenate([tokens] * (128 // tokens.shape[1]), axis=1)
    tokens = pltpu.roll(tokens, (128 - first) % 128, 1)
    vocab = embedding_ref.shape[0]
    onehot = jnp.concatenate(
        [tokens[:, j : j + 1] == lane_iota((L, vocab)) for j in range(peps)], axis=0
    ).astype(BF)
    state = jnp.dot(onehot, embedding_ref[...], preferred_element_type=F32)
    state = state + jnp.concatenate([code_ref[...]] * peps, axis=0)

    tile_lengths = []
    for t in range(STEP // TILE):
        lane = lane_iota((1, TILE)) // L
        vec = jnp.full((1, TILE), lengths_ref[first + t * 4], jnp.int32)
        for j in range(1, TILE // L):
            vec = jnp.where(lane == j, lengths_ref[first + t * 4 + j], vec)
        tile_lengths.append(vec)

    seen = set()

    def waits(layer):
        if layer not in seen:
            seen.add(layer)
            for move in moves[layer]:
                move.wait()

    share = STEP // SHARES
    refs = (w_qkv_ref, w_out_ref, w_up_ref, w_down_ref, gain_ref)
    state = interleave(
        [
            transform(
                state[i * share : (i + 1) * share],
                tile_lengths[i * share // TILE : (i + 1) * share // TILE],
                refs,
                waits,
            )
            for i in range(SHARES)
        ]
    )
    state = jnp.concatenate(state, axis=0)
    normed = norm_rows(state, final_ref[...].reshape(1, D).astype(F32))
    head = jnp.concatenate([w_head_ref[...]] * 4, axis=0)
    logit_ref[...] = lax.dot_general(normed, head, NT, preferred_element_type=F32)

    lane = lane_iota((peps, 128)) // ION
    tiles = []
    for t in range(SPEC // 128):
        tile = logit_ref[pl.ds(4 * t, peps, stride=L), :]
        for i in range(1, 4):
            tile = jnp.where(lane == i, logit_ref[pl.ds(4 * t + i, peps, stride=L), :], tile)
        tiles.append(tile)
    logits = jnp.concatenate(tiles, axis=1)
    intensity = 1.0 / (1.0 + jnp.exp(-logits))
    row = row_iota((peps, 128))
    column = lane_iota((peps, 128))
    length = jnp.zeros((peps, 128), jnp.int32)
    tag = jnp.zeros((peps, 128), jnp.int32)
    for i in range(peps):
        length = jnp.where(row == i, lengths_ref[first + i], length)
        for c, ref in enumerate((towner_ref, tsub_ref, downer_ref, dsub_ref)):
            tag = jnp.where((row == i) & (column == LAST % 128 + 1 + c), ref[first + i], tag)
    position = lane_iota((peps, SPEC)) // ION
    length = jnp.concatenate([length] * (SPEC // 128), axis=1)
    intensity = jnp.where(position < length - 1, intensity, F32(0.0))
    spectra = standardize(intensity)
    rows_ref[:, : SPEC - 128] = spectra[:, : SPEC - 128]
    rows_ref[:, SPEC - 128 :] = jnp.where(
        (column > LAST % 128) & (column <= LAST % 128 + 4),
        tag.astype(F32).astype(BF),
        spectra[:, SPEC - 128 :],
    )


def predict_rows(
    part,
    parts,
    before,
    tokens,
    lengths,
    towner,
    tsub,
    downer,
    dsub,
    embedding,
    w_qkv,
    w_out,
    w_up,
    w_down,
    gains,
    final,
    w_head,
):
    count = tokens.shape[0]
    peps = STEP // L
    assert parts * peps == count
    whole = lambda shape: pl.BlockSpec(shape, lambda i, *_: (0,) * len(shape))
    operands = (
        tokens.T,
        embedding,
        jnp.asarray(sinusoid()),
        w_qkv,
        w_out,
        w_up,
        w_down,
        gains,
        final,
        w_head.T,
    )
    large = (w_qkv, w_out, w_up, w_down)
    in_specs = [
        pl.BlockSpec(memory_space=pltpu.HBM) if operand.ndim == 3 and operand is not gains else whole(operand.shape)
        for operand in operands
    ]
    scalars = (lengths, towner.reshape(count), tsub, downer.reshape(count), dsub)
    aliases = {}
    if before is not None:
        aliases = {len(scalars) + len(operands): 0}
        operands += (before,)
        in_specs += [pl.BlockSpec(memory_space=pl.ANY)]
    grid = pltpu.PrefetchScalarGridSpec(
        num_scalar_prefetch=0,
        grid=(1,),
        in_specs=[pl.BlockSpec(memory_space=pltpu.SMEM)] * len(scalars) + in_specs,
        out_specs=pl.BlockSpec((peps, SPEC), lambda i, *_: (part, 0)),
        scratch_shapes=[pltpu.VMEM((STEP, 128), F32)]
        + [pltpu.VMEM(weight.shape, BF) for weight in large]
        + [pltpu.SemaphoreType.DMA((NL, len(large), PIECES))],
    )
    tokens_here = count * L // parts
    return pl.pallas_call(
        functools.partial(predict_kernel, part * peps),
        grid_spec=grid,
        out_shape=jax.ShapeDtypeStruct((count, SPEC), BF),
        input_output_aliases=aliases,
        compiler_params=pltpu.CompilerParams(vmem_limit_bytes=VMEM_LIMIT),
        cost_estimate=pl.CostEstimate(
            flops=2 * 12 * NL * tokens_here * D * D,
            bytes_accessed=4 * 2**20,
            transcendentals=2 * tokens_here * FF,
        ),
        name="predict",
    )(*scalars, *operands)


def slots_of(bins):
    count = bins.shape[1]
    across = jnp.broadcast_to(bins.astype(F32), (count, count))
    down = across.T
    earlier = (across == down) & (row_iota((count, count)) < lane_iota((count, count)))
    rank = jnp.sum(earlier.astype(F32), axis=0, keepdims=True)
    local = bins.astype(F32) - jnp.min(bins.astype(F32), axis=1, keepdims=True)
    return (local * QPB + rank).astype(jnp.int32)


def query_kernel(copies, bins_ref, spectra_ref, out_ref, ready_ref, sem):
    count = spectra_ref.shape[0]
    place = (row_iota((count, count)) == slots_of(bins_ref[...])).astype(BF)
    ready = standardize(spectra_ref[...].astype(F32))
    ready_ref[...] = jnp.dot(place, ready, preferred_element_type=F32).astype(BF)
    moves = [pltpu.make_async_copy(ready_ref, out_ref.at[i], sem.at[i]) for i in range(copies)]
    for move in moves:
        move.start()
    for move in moves:
        move.wait()


def prepare_queries(query_bin, spectra, copies):
    count = spectra.shape[0]
    return pl.pallas_call(
        functools.partial(query_kernel, copies),
        out_shape=jax.ShapeDtypeStruct((copies,) + spectra.shape, BF),
        out_specs=pl.BlockSpec(memory_space=pltpu.HBM),
        scratch_shapes=[pltpu.VMEM(spectra.shape, BF), pltpu.SemaphoreType.DMA((copies,))],
        compiler_params=pltpu.CompilerParams(vmem_limit_bytes=VMEM_LIMIT),
        name="prepare",
    )(query_bin.reshape(1, count), spectra)


def turn_kernel(mass_ref, *refs):
    sources, (side_ref, subs_ref) = refs[:-2], refs[-2:]
    per = 128 // sources[0].shape[0]
    half = side_ref.shape[1] // 2
    me = mass_ref[0].astype(F32)
    for i in range(len(sources) // per):
        turned = jnp.concatenate([ref[...] for ref in sources[i * per : (i + 1) * per]], axis=0).T
        last = turned[LAST : LAST + 16].astype(F32)
        background = jnp.broadcast_to(last[:1], (ION, 128)).astype(BF)
        targets, decoys = pl.ds(i * 128, 128), pl.ds(half + i * 128, 128)
        side_ref[:LAST, targets] = turned[:LAST]
        side_ref[LAST:, targets] = background
        side_ref[:ION, decoys] = background
        for p in range(1, L):
            side_ref[p * ION : (p + 1) * ION, decoys] = turned[(L - 1 - p) * ION : (L - p) * ION]
        for kind, lanes in enumerate((targets, decoys)):
            owner, sub = last[1 + 2 * kind : 2 + 2 * kind], last[2 + 2 * kind : 3 + 2 * kind]
            sub = jnp.where(owner == me, sub, F32(-1.0))
            subs_ref[:, lanes] = jnp.broadcast_to(sub, (8, 128))


def turn(mass, sources):
    columns = 2 * len(sources) * sources[0].shape[0]
    return pl.pallas_call(
        turn_kernel,
        in_specs=[pl.BlockSpec(memory_space=pltpu.SMEM)]
        + [pl.BlockSpec(memory_space=pltpu.VMEM)] * len(sources),
        out_shape=(
            jax.ShapeDtypeStruct((SPEC, columns), BF),
            jax.ShapeDtypeStruct((8, columns), F32),
        ),
        compiler_params=pltpu.CompilerParams(vmem_limit_bytes=32 * 1024 * 1024),
        cost_estimate=pl.CostEstimate(flops=0, bytes_accessed=4 * 2**20, transcendentals=0),
        name="turn",
    )(mass, *sources)


def score_kernel(ys, zs, jobs, sides, seq_ref, *refs):
    turned, out_ref = refs[: 2 * sides], refs[-1]
    blocks, rest = refs[2 * sides : 2 * sides + len(jobs)], refs[2 * sides + len(jobs) : -1]
    y = lax.div(seq_ref[0], zs)
    low, row = lane_iota((8, 128)) < 32, row_iota((8, 128))
    for (back, which, more), block in zip(jobs, blocks):
        queries = block[...]
        count = queries.shape[0]
        there = lax.rem(y + ys - back, ys)
        bins = (row_iota((count, 128)) // QPB + there * (count // QPB)).astype(F32)
        tops = [jnp.zeros((count, 128), F32) for _ in range(2)]
        for side in which:
            side_ref, subs_ref = turned[2 * side : 2 * side + 2]
            scores = jnp.dot(queries, side_ref[...], preferred_element_type=F32)
            tiles = scores.shape[1] // 128
            for i in range(tiles):
                kind = 2 * i // tiles
                own = jnp.where(
                    subs_ref[:1, i * 128 : (i + 1) * 128] == bins,
                    scores[:, i * 128 : (i + 1) * 128],
                    F32(0.0),
                )
                tops[kind] = jnp.maximum(tops[kind], own)
        best = [jnp.max(top.T, axis=0, keepdims=True) * F32(1.0 / math.sqrt(SPEC)) for top in tops]
        out = jnp.zeros((8, 128), F32)
        for z in range(zs):
            tile, shift = z // 4, 32 * (z % 4)
            pair = [jnp.broadcast_to(b[:, tile * 128 : (tile + 1) * 128], (8, 128)) for b in best]
            near = pltpu.roll(pair[0], (128 - shift) % 128, 1)
            far = pltpu.roll(pair[1], (128 - shift + 32) % 128, 1)
            out = jnp.where(row == z, jnp.where(low, near, far), out)
        place = pl.ds(pl.multiple_of(there * zs, 8), zs)
        if more:
            out = jnp.maximum(out, rest[0][place, :])
        out_ref[place, :] = out


def score(ys, zs, seq, sides, blocks, jobs, rest=()):
    inside = pl.BlockSpec(memory_space=pltpu.VMEM)
    used = [blocks[job[0]] for job in jobs]
    return pl.pallas_call(
        functools.partial(score_kernel, ys, zs, jobs, len(sides)),
        in_specs=[pl.BlockSpec(memory_space=pltpu.SMEM)]
        + [inside] * (2 * len(sides) + len(used) + len(rest)),
        out_specs=inside,
        out_shape=jax.ShapeDtypeStruct((ys * zs, 128), F32),
        compiler_params=pltpu.CompilerParams(vmem_limit_bytes=32 * 1024 * 1024),
        name="score",
    )(seq, *[part for side in sides for part in side], *used, *rest)


def finish_kernel(bins_ref, pieces_ref, target_ref, decoy_ref):
    count = bins_ref.shape[1]
    best = jnp.maximum(jnp.max(pieces_ref[...], axis=0, keepdims=True), F32(0.0))
    slots = slots_of(bins_ref[...])
    place = row_iota((count, count)) == slots
    for kind, ref in enumerate((target_ref, decoy_ref)):
        wide = jnp.broadcast_to(best[:, kind * count : (kind + 1) * count], (count, count)).T
        ref[...] = jnp.sum(jnp.where(place, wide, F32(0.0)), axis=0, keepdims=True)


def finish(query_bin, pieces):
    count = query_bin.shape[0]
    shape = jax.ShapeDtypeStruct((1, count), F32)
    target, decoy = pl.pallas_call(finish_kernel, out_shape=(shape, shape), name="finish")(
        query_bin.reshape(1, count), pieces
    )
    return target.reshape(count), decoy.reshape(count)


def local(
    peptide_tokens,
    peptide_lengths,
    target_owner,
    target_sub,
    decoy_owner,
    decoy_sub,
    embedding,
    w_qkv,
    w_out,
    w_up,
    w_down,
    layer_gain,
    final_gain,
    w_head,
    query_spectra,
    query_bin,
):
    seqs = lax.axis_size("seq")
    ys, zs = YS, seqs // YS
    along_z = [[y * zs + z for z in range(zs)] for y in range(ys)]
    weights = (embedding, w_qkv, w_out, w_up, w_down, layer_gain, final_gain, w_head)
    owners = (target_owner, target_sub, decoy_owner, decoy_sub)
    queries = prepare_queries(query_bin, query_spectra, zs)
    queries = lax.all_to_all(
        queries, "seq", split_axis=0, concat_axis=0, tiled=True, axis_index_groups=along_z
    ).reshape(-1, SPEC)
    rows = predict_rows(0, 2, None, peptide_tokens, peptide_lengths, *owners, *weights)
    queries, rows, peptide_lengths = lax.optimization_barrier((queries, rows, peptide_lengths))
    ahead, back = [[(i, (i + d * zs) % seqs) for i in range(seqs)] for d in (1, ys - 1)]
    blocks = [queries, lax.ppermute(queries, "seq", ahead), None, lax.ppermute(queries, "seq", back)]
    rows = predict_rows(1, 2, rows, peptide_tokens, peptide_lengths, *owners, *weights)
    rows, blocks[1], blocks[3] = lax.optimization_barrier((rows, blocks[1], blocks[3]))
    blocks[2] = lax.ppermute(blocks[1], "seq", ahead)
    masses = lax.axis_size("mass")
    swap = [(i, i ^ 1) for i in range(masses)]
    far = [
        lax.ppermute(rows, "mass", [(i, (i + d) % masses) for i in range(masses)])
        for d in range(2, masses, 2)
    ]
    mass, seq = [lax.axis_index(axis).astype(jnp.int32).reshape(1) for axis in ("mass", "seq")]
    near = [rows, lax.ppermute(rows, "mass", swap), far[0], lax.ppermute(far[0], "mass", swap)]
    near = turn(mass, near)
    half = score(ys, zs, seq, [near], blocks, [(0, (0,), False), (1, (0,), False), (3, (0,), False)])
    far = turn(mass, far[1:] + [lax.ppermute(part, "mass", swap) for part in far[1:]])
    jobs = [(0, (1,), True), (1, (1,), True), (2, (0, 1), False), (3, (1,), True)]
    pieces = score(ys, zs, seq, [near, far], blocks, jobs, [half])[:, None, :]
    pieces = lax.all_to_all(pieces, "seq", split_axis=0, concat_axis=0, tiled=True)[:, 0, :]
    return finish(query_bin, pieces)


def solution(mesh):
    in_specs = (
        P(("mass", "seq"), None),
        P(("mass", "seq")),
        P(("mass", "seq"), None),
        P(("mass", "seq")),
        P(("mass", "seq"), None),
        P(("mass", "seq")),
        P(),
        P(),
        P(),
        P(),
        P(),
        P(),
        P(),
        P(),
        P(("mass", "seq"), None),
        P(("mass", "seq")),
    )
    out_specs = (P(("mass", "seq")), P(("mass", "seq")))
    return jax.shard_map(local, mesh=mesh, in_specs=in_specs, out_specs=out_specs, check_vma=False)
```

```python
import functools
import math

import jax
import jax.numpy as jnp
import numpy as np
from jax import lax
from jax.experimental import pallas as pl
from jax.experimental.pallas import tpu as pltpu
from jax.sharding import PartitionSpec as P

HEADS = 8
L = 32
ION = 32
NL = 2
QPB = 4
YS = 4
D = 256
FF = 1024
SPEC = L * ION
EPS = 1e-06
BF = jnp.bfloat16
F32 = jnp.float32

STEP = 1024
TILE = 128
GROUP = 8
PIECES = 1
SHARES = 2
LAG = 0
LAST = SPEC - ION
VMEM_LIMIT = 60 * 1024 * 1024
NT = (((1,), (1,)), ((), ()))


def sinusoid():
    place = np.arange(L, dtype=np.float32)[:, None]
    index = np.arange(D // 2, dtype=np.float32)[None, :]
    angle = place * np.exp(-math.log(10000.0) * 2.0 * index / D).astype(np.float32)
    return np.concatenate([np.sin(angle), np.cos(angle)], axis=1).astype(np.float32)


def lane_iota(shape):
    return lax.broadcasted_iota(jnp.int32, shape, len(shape) - 1)


def row_iota(shape):
    return lax.broadcasted_iota(jnp.int32, shape, len(shape) - 2)


def norm_rows(values, gain):
    scale = lax.rsqrt(jnp.mean(values * values, axis=-1, keepdims=True) + EPS)
    return (values * scale * gain).astype(BF)


def standardize(spectra):
    centred = spectra - jnp.mean(spectra, axis=-1, keepdims=True)
    return (centred * lax.rsqrt(jnp.mean(centred * centred, axis=-1, keepdims=True) + EPS)).astype(BF)


def gelu(x):
    inner = x * (math.sqrt(2 / math.pi) + (math.sqrt(2 / math.pi) * 0.044715) * (x * x))
    half = 0.5 * x
    return half + half * jnp.tanh(inner)


def feed_forward(state, normed, w_up_ref, w_down_ref):
    for c in range(0, FF, D):
        up = jnp.dot(normed, w_up_ref[:, c : c + D], preferred_element_type=F32)
        hidden = gelu(up).astype(BF)
        state = state + jnp.dot(hidden, w_down_ref[c : c + D, :], preferred_element_type=F32)
        yield
    return state


def attend(items):
    heads, peps = TILE // L, TILE // L
    lane = (lane_iota((L, heads * TILE)) % TILE) // L
    empty = jnp.zeros((L, TILE), BF)
    scores = []
    for query, key, _, _ in items:
        turned = query.T
        spread = [
            jnp.concatenate(
                [turned[h * L : (h + 1) * L] if h == i else empty for i in range(heads)], axis=1
            )
            for h in range(heads)
        ]
        spread = jnp.concatenate(spread, axis=0)
        scores.append(jnp.dot(key, spread, preferred_element_type=F32))
    yield
    wide = []
    for score, (_, _, _, length) in zip(scores, items):
        own = score[:L]
        for j in range(1, peps):
            own = jnp.where(lane == j, score[j * L : (j + 1) * L], own)
        own = own * (1.0 / math.sqrt(L))
        own = jnp.where(
            row_iota(own.shape) < jnp.concatenate([length] * heads, axis=1), own, F32(-1e30)
        )
        weights = jnp.exp(own - jnp.max(own, axis=0, keepdims=True))
        probs = weights * (1.0 / jnp.sum(weights, axis=0, keepdims=True))
        probs = probs.astype(BF)
        wide.append(
            jnp.concatenate(
                [jnp.where(lane == j, probs, jnp.zeros_like(probs)) for j in range(peps)], axis=0
            )
        )
    yield
    heard = []
    for probs, (_, _, value, _) in zip(wide, items):
        turned = value.T
        heard.append(
            jnp.concatenate(
                [
                    jnp.dot(
                        turned[h * L : (h + 1) * L],
                        probs[:, h * TILE : (h + 1) * TILE],
                        preferred_element_type=F32,
                    )
                    for h in range(heads)
                ],
                axis=0,
            )
        )
    yield
    return [out.T.astype(BF) for out in heard]


def transform(state, tile_lengths, refs, waits):
    w_qkv_ref, w_out_ref, w_up_ref, w_down_ref, gain_ref = refs
    for layer in range(NL):
        normed = norm_rows(state, gain_ref[layer, 0:1, :].astype(F32))
        waits(layer)
        mixed = [
            jnp.dot(
                normed, w_qkv_ref[layer, :, c * D : (c + 1) * D], preferred_element_type=F32
            ).astype(BF)
            for c in range(3)
        ]
        yield
        items = [
            [m[t * TILE : (t + 1) * TILE, g * TILE : (g + 1) * TILE] for m in mixed] + [tile_lengths[t]]
            for t in range(state.shape[0] // TILE)
            for g in range(D // TILE)
        ]
        heard = []
        for i in range(0, len(items), GROUP):
            heard = heard + (yield from attend(items[i : i + GROUP]))
        attended = jnp.concatenate(
            [jnp.concatenate(heard[i : i + 2], axis=1) for i in range(0, len(heard), 2)], axis=0
        )
        state = state + jnp.dot(attended, w_out_ref[layer], preferred_element_type=F32)
        normed = norm_rows(state, gain_ref[layer, 1:2, :].astype(F32))
        yield
        state = yield from feed_forward(state, normed, w_up_ref.at[layer], w_down_ref.at[layer])
    return state


def interleave(shares):
    results, step = [None] * len(shares), 0
    running = list(range(len(shares)))
    while running:
        for i in list(running):
            if step >= i * LAG:
                try:
                    next(shares[i])
                except StopIteration as stop:
                    results[i] = stop.value
                    running.remove(i)
        step += 1
    return results


def predict_kernel(
    base,
    lengths_ref,
    towner_ref,
    tsub_ref,
    downer_ref,
    dsub_ref,
    tokens_ref,
    embedding_ref,
    code_ref,
    w_qkv_ref,
    w_out_ref,
    w_up_ref,
    w_down_ref,
    gain_ref,
    final_ref,
    w_head_ref,
    *refs,
):
    rows_ref, logit_ref, sems = refs[-7], refs[-6], refs[-1]
    peps = STEP // L
    sources = (w_qkv_ref, w_out_ref, w_up_ref, w_down_ref)
    kept = refs[-5:-1]
    moves = [
        [
            pltpu.make_async_copy(
                source.at[layer, pl.ds(p * source.shape[1] // PIECES, source.shape[1] // PIECES)],
                held.at[layer, pl.ds(p * source.shape[1] // PIECES, source.shape[1] // PIECES)],
                sems.at[layer, i, p],
            )
            for i, (source, held) in enumerate(zip(sources, kept))
            for p in range(PIECES)
        ]
        for layer in range(NL)
    ]
    w_qkv_ref, w_out_ref, w_up_ref, w_down_ref = kept
    for move in moves[0] + moves[1]:
        move.start()

    first = base
    tokens = tokens_ref[...]
    tokens = jnp.concatenate([tokens] * (128 // tokens.shape[1]), axis=1)
    tokens = pltpu.roll(tokens, (128 - first) % 128, 1)
    vocab = embedding_ref.shape[0]
    onehot = jnp.concatenate(
        [tokens[:, j : j + 1] == lane_iota((L, vocab)) for j in range(peps)], axis=0
    ).astype(BF)
    state = jnp.dot(onehot, embedding_ref[...], preferred_element_type=F32)
    state = state + jnp.concatenate([code_ref[...]] * peps, axis=0)

    tile_lengths = []
    for t in range(STEP // TILE):
        lane = lane_iota((1, TILE)) // L
        vec = jnp.full((1, TILE), lengths_ref[first + t * 4], jnp.int32)
        for j in range(1, TILE // L):
            vec = jnp.where(lane == j, lengths_ref[first + t * 4 + j], vec)
        tile_lengths.append(vec)

    seen = set()

    def waits(layer):
        if layer not in seen:
            seen.add(layer)
            for move in moves[layer]:
                move.wait()

    share = STEP // SHARES
    refs = (w_qkv_ref, w_out_ref, w_up_ref, w_down_ref, gain_ref)
    state = interleave(
        [
            transform(
                state[i * share : (i + 1) * share],
                tile_lengths[i * share // TILE : (i + 1) * share // TILE],
                refs,
                waits,
            )
            for i in range(SHARES)
        ]
    )
    state = jnp.concatenate(state, axis=0)
    normed = norm_rows(state, final_ref[...].reshape(1, D).astype(F32))
    head = jnp.concatenate([w_head_ref[...]] * 4, axis=0)
    logit_ref[...] = lax.dot_general(normed, head, NT, preferred_element_type=F32)

    lane = lane_iota((peps, 128)) // ION
    tiles = []
    for t in range(SPEC // 128):
        tile = logit_ref[pl.ds(4 * t, peps, stride=L), :]
        for i in range(1, 4):
            tile = jnp.where(lane == i, logit_ref[pl.ds(4 * t + i, peps, stride=L), :], tile)
        tiles.append(tile)
    logits = jnp.concatenate(tiles, axis=1)
    intensity = 1.0 / (1.0 + jnp.exp(-logits))
    row = row_iota((peps, 128))
    column = lane_iota((peps, 128))
    length = jnp.zeros((peps, 128), jnp.int32)
    tag = jnp.zeros((peps, 128), jnp.int32)
    for i in range(peps):
        length = jnp.where(row == i, lengths_ref[first + i], length)
        for c, ref in enumerate((towner_ref, tsub_ref, downer_ref, dsub_ref)):
            tag = jnp.where((row == i) & (column == LAST % 128 + 1 + c), ref[first + i], tag)
    position = lane_iota((peps, SPEC)) // ION
    length = jnp.concatenate([length] * (SPEC // 128), axis=1)
    intensity = jnp.where(position < length - 1, intensity, F32(0.0))
    spectra = standardize(intensity)
    rows_ref[:, : SPEC - 128] = spectra[:, : SPEC - 128]
    rows_ref[:, SPEC - 128 :] = jnp.where(
        (column > LAST % 128) & (column <= LAST % 128 + 4),
        tag.astype(F32).astype(BF),
        spectra[:, SPEC - 128 :],
    )


def predict_rows(
    part,
    parts,
    before,
    tokens,
    lengths,
    towner,
    tsub,
    downer,
    dsub,
    embedding,
    w_qkv,
    w_out,
    w_up,
    w_down,
    gains,
    final,
    w_head,
):
    count = tokens.shape[0]
    peps = STEP // L
    assert parts * peps == count
    whole = lambda shape: pl.BlockSpec(shape, lambda i, *_: (0,) * len(shape))
    operands = (
        tokens.T,
        embedding,
        jnp.asarray(sinusoid()),
        w_qkv,
        w_out,
        w_up,
        w_down,
        gains,
        final,
        w_head.T,
    )
    large = (w_qkv, w_out, w_up, w_down)
    in_specs = [
        pl.BlockSpec(memory_space=pltpu.HBM) if operand.ndim == 3 and operand is not gains else whole(operand.shape)
        for operand in operands
    ]
    scalars = (lengths, towner.reshape(count), tsub, downer.reshape(count), dsub)
    aliases = {}
    if before is not None:
        aliases = {len(scalars) + len(operands): 0}
        operands += (before,)
        in_specs += [pl.BlockSpec(memory_space=pl.ANY)]
    grid = pltpu.PrefetchScalarGridSpec(
        num_scalar_prefetch=0,
        grid=(1,),
        in_specs=[pl.BlockSpec(memory_space=pltpu.SMEM)] * len(scalars) + in_specs,
        out_specs=pl.BlockSpec((peps, SPEC), lambda i, *_: (part, 0)),
        scratch_shapes=[pltpu.VMEM((STEP, 128), F32)]
        + [pltpu.VMEM(weight.shape, BF) for weight in large]
        + [pltpu.SemaphoreType.DMA((NL, len(large), PIECES))],
    )
    tokens_here = count * L // parts
    return pl.pallas_call(
        functools.partial(predict_kernel, part * peps),
        grid_spec=grid,
        out_shape=jax.ShapeDtypeStruct((count, SPEC), BF),
        input_output_aliases=aliases,
        compiler_params=pltpu.CompilerParams(vmem_limit_bytes=VMEM_LIMIT),
        cost_estimate=pl.CostEstimate(
            flops=2 * 12 * NL * tokens_here * D * D,
            bytes_accessed=4 * 2**20,
            transcendentals=2 * tokens_here * FF,
        ),
        name="predict",
    )(*scalars, *operands)


def slots_of(bins):
    count = bins.shape[1]
    across = jnp.broadcast_to(bins.astype(F32), (count, count))
    down = across.T
    earlier = (across == down) & (row_iota((count, count)) < lane_iota((count, count)))
    rank = jnp.sum(earlier.astype(F32), axis=0, keepdims=True)
    local = bins.astype(F32) - jnp.min(bins.astype(F32), axis=1, keepdims=True)
    return (local * QPB + rank).astype(jnp.int32)


def query_kernel(copies, bins_ref, spectra_ref, out_ref, ready_ref, sem):
    count = spectra_ref.shape[0]
    place = (row_iota((count, count)) == slots_of(bins_ref[...])).astype(BF)
    ready = standardize(spectra_ref[...].astype(F32))
    ready_ref[...] = jnp.dot(place, ready, preferred_element_type=F32).astype(BF)
    moves = [pltpu.make_async_copy(ready_ref, out_ref.at[i], sem.at[i]) for i in range(copies)]
    for move in moves:
        move.start()
    for move in moves:
        move.wait()


def prepare_queries(query_bin, spectra, copies):
    count = spectra.shape[0]
    return pl.pallas_call(
        functools.partial(query_kernel, copies),
        out_shape=jax.ShapeDtypeStruct((copies,) + spectra.shape, BF),
        out_specs=pl.BlockSpec(memory_space=pltpu.HBM),
        scratch_shapes=[pltpu.VMEM(spectra.shape, BF), pltpu.SemaphoreType.DMA((copies,))],
        compiler_params=pltpu.CompilerParams(vmem_limit_bytes=VMEM_LIMIT),
        name="prepare",
    )(query_bin.reshape(1, count), spectra)


def turn_kernel(mass_ref, *refs):
    sources, (side_ref, subs_ref) = refs[:-2], refs[-2:]
    per = 128 // sources[0].shape[0]
    half = side_ref.shape[1] // 2
    me = mass_ref[0].astype(F32)
    for i in range(len(sources) // per):
        turned = jnp.concatenate([ref[...] for ref in sources[i * per : (i + 1) * per]], axis=0).T
        last = turned[LAST : LAST + 16].astype(F32)
        background = jnp.broadcast_to(last[:1], (ION, 128)).astype(BF)
        targets, decoys = pl.ds(i * 128, 128), pl.ds(half + i * 128, 128)
        side_ref[:LAST, targets] = turned[:LAST]
        side_ref[LAST:, targets] = background
        side_ref[:ION, decoys] = background
        for p in range(1, L):
            side_ref[p * ION : (p + 1) * ION, decoys] = turned[(L - 1 - p) * ION : (L - p) * ION]
        for kind, lanes in enumerate((targets, decoys)):
            owner, sub = last[1 + 2 * kind : 2 + 2 * kind], last[2 + 2 * kind : 3 + 2 * kind]
            sub = jnp.where(owner == me, sub, F32(-1.0))
            subs_ref[:, lanes] = jnp.broadcast_to(sub, (8, 128))


def turn(mass, sources):
    columns = 2 * len(sources) * sources[0].shape[0]
    return pl.pallas_call(
        turn_kernel,
        in_specs=[pl.BlockSpec(memory_space=pltpu.SMEM)]
        + [pl.BlockSpec(memory_space=pltpu.VMEM)] * len(sources),
        out_shape=(
            jax.ShapeDtypeStruct((SPEC, columns), BF),
            jax.ShapeDtypeStruct((8, columns), F32),
        ),
        compiler_params=pltpu.CompilerParams(vmem_limit_bytes=32 * 1024 * 1024),
        cost_estimate=pl.CostEstimate(flops=0, bytes_accessed=4 * 2**20, transcendentals=0),
        name="turn",
    )(mass, *sources)


def score_kernel(ys, zs, jobs, sides, seq_ref, *refs):
    turned, out_ref = refs[: 2 * sides], refs[-1]
    blocks, rest = refs[2 * sides : 2 * sides + len(jobs)], refs[2 * sides + len(jobs) : -1]
    y = lax.div(seq_ref[0], zs)
    low, row = lane_iota((8, 128)) < 32, row_iota((8, 128))
    for (back, which, more), block in zip(jobs, blocks):
        queries = block[...]
        count = queries.shape[0]
        there = lax.rem(y + ys - back, ys)
        bins = (row_iota((count, 128)) // QPB + there * (count // QPB)).astype(F32)
        tops = [jnp.zeros((count, 128), F32) for _ in range(2)]
        for side in which:
            side_ref, subs_ref = turned[2 * side : 2 * side + 2]
            scores = jnp.dot(queries, side_ref[...], preferred_element_type=F32)
            tiles = scores.shape[1] // 128
            for i in range(tiles):
                kind = 2 * i // tiles
                own = jnp.where(
                    subs_ref[:1, i * 128 : (i + 1) * 128] == bins,
                    scores[:, i * 128 : (i + 1) * 128],
                    F32(0.0),
                )
                tops[kind] = jnp.maximum(tops[kind], own)
        best = [jnp.max(top.T, axis=0, keepdims=True) * F32(1.0 / math.sqrt(SPEC)) for top in tops]
        out = jnp.zeros((8, 128), F32)
        for z in range(zs):
            tile, shift = z // 4, 32 * (z % 4)
            pair = [jnp.broadcast_to(b[:, tile * 128 : (tile + 1) * 128], (8, 128)) for b in best]
            near = pltpu.roll(pair[0], (128 - shift) % 128, 1)
            far = pltpu.roll(pair[1], (128 - shift + 32) % 128, 1)
            out = jnp.where(row == z, jnp.where(low, near, far), out)
        place = pl.ds(pl.multiple_of(there * zs, 8), zs)
        if more:
            out = jnp.maximum(out, rest[0][place, :])
        out_ref[place, :] = out


def score(ys, zs, seq, sides, blocks, jobs, rest=()):
    inside = pl.BlockSpec(memory_space=pltpu.VMEM)
    used = [blocks[job[0]] for job in jobs]
    return pl.pallas_call(
        functools.partial(score_kernel, ys, zs, jobs, len(sides)),
        in_specs=[pl.BlockSpec(memory_space=pltpu.SMEM)]
        + [inside] * (2 * len(sides) + len(used) + len(rest)),
        out_specs=inside,
        out_shape=jax.ShapeDtypeStruct((ys * zs, 128), F32),
        compiler_params=pltpu.CompilerParams(vmem_limit_bytes=32 * 1024 * 1024),
        cost_estimate=pl.CostEstimate(
            flops=sum(2 * blocks[0].size * sides[i][0].shape[1] for job in jobs for i in job[1]),
            bytes_accessed=4 * 2**20,
            transcendentals=0,
        ),
        name="score",
    )(seq, *[part for side in sides for part in side], *used, *rest)


def finish_kernel(bins_ref, pieces_ref, target_ref, decoy_ref):
    count = bins_ref.shape[1]
    best = jnp.maximum(jnp.max(pieces_ref[...], axis=0, keepdims=True), F32(0.0))
    slots = slots_of(bins_ref[...])
    place = row_iota((count, count)) == slots
    for kind, ref in enumerate((target_ref, decoy_ref)):
        wide = jnp.broadcast_to(best[:, kind * count : (kind + 1) * count], (count, count)).T
        ref[...] = jnp.sum(jnp.where(place, wide, F32(0.0)), axis=0, keepdims=True)


def finish(query_bin, pieces):
    count = query_bin.shape[0]
    shape = jax.ShapeDtypeStruct((1, count), F32)
    target, decoy = pl.pallas_call(finish_kernel, out_shape=(shape, shape), name="finish")(
        query_bin.reshape(1, count), pieces
    )
    return target.reshape(count), decoy.reshape(count)


def local(
    peptide_tokens,
    peptide_lengths,
    target_owner,
    target_sub,
    decoy_owner,
    decoy_sub,
    embedding,
    w_qkv,
    w_out,
    w_up,
    w_down,
    layer_gain,
    final_gain,
    w_head,
    query_spectra,
    query_bin,
):
    seqs = lax.axis_size("seq")
    ys, zs = YS, seqs // YS
    along_z = [[y * zs + z for z in range(zs)] for y in range(ys)]
    weights = (embedding, w_qkv, w_out, w_up, w_down, layer_gain, final_gain, w_head)
    owners = (target_owner, target_sub, decoy_owner, decoy_sub)
    queries = prepare_queries(query_bin, query_spectra, zs)
    queries = lax.all_to_all(
        queries, "seq", split_axis=0, concat_axis=0, tiled=True, axis_index_groups=along_z
    ).reshape(-1, SPEC)
    rows = predict_rows(0, 2, None, peptide_tokens, peptide_lengths, *owners, *weights)
    queries, rows, peptide_lengths = lax.optimization_barrier((queries, rows, peptide_lengths))
    ahead, back = [[(i, (i + d * zs) % seqs) for i in range(seqs)] for d in (1, ys - 1)]
    blocks = [queries, lax.ppermute(queries, "seq", ahead), None, lax.ppermute(queries, "seq", back)]
    rows = predict_rows(1, 2, rows, peptide_tokens, peptide_lengths, *owners, *weights)
    rows, blocks[1], blocks[3] = lax.optimization_barrier((rows, blocks[1], blocks[3]))
    blocks[2] = lax.ppermute(blocks[1], "seq", ahead)
    masses = lax.axis_size("mass")
    swap = [(i, i ^ 1) for i in range(masses)]
    far = [
        lax.ppermute(rows, "mass", [(i, (i + d) % masses) for i in range(masses)])
        for d in range(2, masses, 2)
    ]
    mass, seq = [lax.axis_index(axis).astype(jnp.int32).reshape(1) for axis in ("mass", "seq")]
    near = [rows, lax.ppermute(rows, "mass", swap), far[0], lax.ppermute(far[0], "mass", swap)]
    near = turn(mass, near)
    half = score(ys, zs, seq, [near], blocks, [(0, (0,), False), (1, (0,), False), (3, (0,), False)])
    far = turn(mass, far[1:] + [lax.ppermute(part, "mass", swap) for part in far[1:]])
    jobs = [(0, (1,), True), (1, (1,), True), (2, (0, 1), False), (3, (1,), True)]
    pieces = score(ys, zs, seq, [near, far], blocks, jobs, [half])[:, None, :]
    pieces = lax.all_to_all(pieces, "seq", split_axis=0, concat_axis=0, tiled=True)[:, 0, :]
    return finish(query_bin, pieces)


def solution(mesh):
    in_specs = (
        P(("mass", "seq"), None),
        P(("mass", "seq")),
        P(("mass", "seq"), None),
        P(("mass", "seq")),
        P(("mass", "seq"), None),
        P(("mass", "seq")),
        P(),
        P(),
        P(),
        P(),
        P(),
        P(),
        P(),
        P(),
        P(("mass", "seq"), None),
        P(("mass", "seq")),
    )
    out_specs = (P(("mass", "seq")), P(("mass", "seq")))
    return jax.shard_map(local, mesh=mesh, in_specs=in_specs, out_specs=out_specs, check_vma=False)
```
